32 devices in a mesh: dp: 4 (over z), expert: 8 (over y, x, core).
Axes of the slice: x: 2, y: 2, z: 4, core: 2. Of those that a mesh axis runs over, the one named last changes fastest.
Arguments:
- cotangent: bfloat16 [4096, 2048], P(('dp', 'expert')), may hold values from -6 to 6
- saved_gate_up: bfloat16 [4096, 8, 1536], P(('dp', 'expert')), may hold values from -6 to 6
- route_ids: int32 [4096, 8], P(('dp', 'expert')), may hold values from 0 to 15, all different within a row; in each aligned block of 128 rows (0 to 127, 128 to 255, ...) at most 128 rows name the same one
- route_weights: float32 [4096, 8], P(('dp', 'expert')), may hold values from 0.05 to 1
- w_down: bfloat16 [16, 768, 2048], P('expert', 'dp'), may hold values from -0.21875 to 0.21875
Outputs:
- grad_gate_up: bfloat16 [4096, 8, 1536], P(('dp', 'expert'))
- route_grad: float32 [4096, 8], P(('dp', 'expert'))
- grad_down: float32 [16, 768, 2048], P('expert', 'dp')
The draws below stay inside these ranges and needn't reach their ends.
Inputs may be any that keep to these rules, and one draw needn't show every extreme that they name: `route_ids`: within the rows of one device (aligned blocks of 128 tokens), no expert is named by more than 128 routes, and in every draw some expert is named by exactly 128; the 8 experts of a token are distinct.
All inputs are finite; a program needn't handle non-finite values.
Results may differ from the reference program's by a relative error of at most 0.02.
Values may be sent and summed in bfloat16 or wider, within the bound.
No kernel may reach another device: no remote copies, remote signals or barrier semaphores. Data moves between devices by JAX's collectives and lax.ppermute only.
A program may use at most 128 MiB of HBM per device.

```python
import math
import jax
import jax.numpy as jnp
import numpy as np
from jax import lax

D = 2048
FF = 768
TOP = 8
TOK_DEV = 128
EXPERTS = 16
CAP = 128
TOKENS = 4096
N_DP = 4
N_EXPERT = 8


def steps_of(own_key, dims, pieces, smallest, high):
    gain = 1.0
    for dim, blocks in pieces:
        draws = jax.random.uniform(jax.random.fold_in(jax.random.fold_in(own_key, 6), dim), (blocks,), jnp.float32, smallest / len(pieces), high / len(pieces))
        gain = gain * jnp.repeat(jnp.exp(draws), dims[dim] // blocks).reshape((-1,) + (1,) * (len(dims) - 1 - dim))
    return gain


def assign_block(rng, own, number, rows, amount, top, bound, skew):
    order = jax.random.permutation(rng, amount)
    heavy_load, common = shares(amount, rows * top, bound, skew, True), shares(amount, rows * top, bound, skew, False)
    places = jnp.arange(amount)

    def named(sizes, offset_by):
        used = int((sizes > 0).sum())
        fixed = max(1, used // 4)
        shifted = fixed + (places - fixed + offset_by * (used - fixed)) % max(1, amount - fixed)
        return jnp.zeros((amount,), jnp.int32).at[order[jnp.where(places < fixed, places, shifted)]].set(jnp.asarray(sizes, jnp.int32))

    sizes = jnp.where(number % 4 == 0, named(heavy_load, number // 4), named(common, number - number // 4 - 1))
    mixed = jax.random.permutation(jax.random.fold_in(own, 3), amount)
    source_of, taker = mixed[0:amount // 2 * 2:2], mixed[1:amount // 2 * 2:2]
    margin = jnp.minimum(sizes[source_of] - 1, bound - sizes[taker]) // 2
    margin = jnp.where((source_of == order[0]) | (taker == order[0]) | (sizes[taker] == 0), 0, jnp.maximum(margin, 0))
    shifted = jax.random.randint(jax.random.fold_in(own, 4), (amount // 2,), 0, 1 << 20) % (margin + 1)
    sizes = sizes.at[source_of].add(-shifted).at[taker].add(shifted)
    items = jnp.searchsorted(jnp.cumsum(sizes), jnp.arange(rows * top), side="right").astype(jnp.int32)
    grid = items.reshape(top, rows).T
    grid = grid[jax.random.permutation(jax.random.fold_in(own, 1), rows)]
    offset_by = jax.random.randint(jax.random.fold_in(own, 2), (rows, 1), 0, top)
    return jnp.take_along_axis(grid, (jnp.arange(top)[None, :] + offset_by) % top, axis=1)


def shares(count, total, limit, skew, full):
    weights = [(1 << 20) // math.isqrt(grade ** skew) + 1 for grade in range(1, count + 1)]
    largest = limit if full else min(limit, max(-(-total // count), total * weights[0] // sum(weights)))
    least = 1 if total - largest >= count - 1 else 0
    given, spare = [largest] + [least] * (count - 1), total - largest - least * (count - 1)
    while spare > 0:
        candidates = [i for i in range(1, count) if given[i] < largest] or [i for i in range(1, count) if given[i] < limit]
        whole, left = sum([weights[i] for i in candidates]), spare
        for i in candidates:
            addition = min(limit - given[i], max(1, left * weights[i] // whole), spare)
            given[i] = given[i] + addition
            spare = spare - addition
    return np.array(given)


def centred(stream_key, shape, spread, bound, cuts=(), held_as=jnp.bfloat16):
    factor_of = steps_of(stream_key, shape, cuts, -0.22, 0.18) if cuts else 1.0
    values = jax.random.normal(stream_key, shape, jnp.float32) * spread * factor_of
    return jnp.minimum(jnp.maximum(values, -bound), bound).astype(held_as)


def setup_inputs(seed: int = 0) -> dict:
    key_list = jax.random.split(jax.random.key(seed), 6)
    cotangent = centred(key_list[0], (TOKENS, D), 1.0, 6.0, ((0, 32),))
    saved_gate_up = centred(key_list[1], (TOKENS, TOP, 2 * FF), 1.0, 6.0, ((0, 32),))
    route_ids_keys = jax.random.split(jax.random.fold_in(key_list[2], 1), TOKENS // TOK_DEV)
    route_ids_turns = jax.random.permutation(jax.random.fold_in(key_list[2], 3), TOKENS // TOK_DEV)
    route_ids = jax.vmap(lambda own, number: assign_block(jax.random.fold_in(key_list[2], 2), own, number, TOK_DEV, EXPERTS, TOP, CAP, 2))(route_ids_keys, route_ids_turns).reshape((TOKENS, TOP))
    route_weights = jnp.clip(jnp.exp(math.log(1.0) - 2.9957323 * jax.random.uniform(key_list[3], (TOKENS, TOP), jnp.float32) ** steps_of(key_list[3], (TOKENS, TOP), ((0, 32),), -0.2, 0.2)), 0.05, 1.0)
    w_down = centred(key_list[4], (EXPERTS, FF, D), FF ** -0.5, 0.21875, ((0, 8), (1, 4)))
    return {"cotangent": cotangent, "saved_gate_up": saved_gate_up, "route_ids": route_ids, "route_weights": route_weights, "w_down": w_down}


def slot_positions(flat_ids, experts, capacity):
    onehot = (flat_ids[:, None] == jnp.arange(experts, dtype=jnp.int32)[None, :]).astype(jnp.int32)
    before = jnp.cumsum(onehot, axis=0) - onehot
    slot = jnp.sum(before * onehot, axis=1).astype(jnp.int32)
    return (flat_ids * capacity + slot).astype(jnp.int32)


def reference(cotangent, saved_gate_up, route_ids, route_weights, w_down):
    devices = N_DP * N_EXPERT
    routes = TOK_DEV * TOP
    total = TOKENS * TOP
    gate = saved_gate_up[:, :, :FF].astype(jnp.float32)
    up = saved_gate_up[:, :, FF:].astype(jnp.float32)
    sig = jax.nn.sigmoid(gate)
    act = gate * sig
    hidden = (act * up).astype(jnp.bfloat16)
    weights = route_weights[:, :, None]
    scaled = (weights * hidden.astype(jnp.float32)).astype(jnp.bfloat16)
    ids = route_ids.reshape(devices, routes)
    position = jax.vmap(lambda row: slot_positions(row, EXPERTS, CAP))(ids)
    global_index = (jnp.arange(devices, dtype=jnp.int32)[:, None] * routes
                    + jnp.arange(routes, dtype=jnp.int32)[None, :]).astype(jnp.int32)
    table = jnp.full((devices, EXPERTS * CAP), total, jnp.int32)
    table = table.at[jnp.arange(devices, dtype=jnp.int32)[:, None], position].set(global_index)
    table = table.reshape(devices, EXPERTS, CAP).transpose(1, 0, 2).reshape(EXPERTS, devices * CAP)
    dy_ext = jnp.concatenate([cotangent, jnp.zeros((1, D), cotangent.dtype)], 0)
    h_ext = jnp.concatenate([scaled.reshape(total, FF), jnp.zeros((1, FF), scaled.dtype)], 0)

    def per_expert(carry, inputs):
        index, weight = inputs
        dy_rows = dy_ext[index // TOP]
        h_rows = h_ext[index]
        grads = jnp.dot(dy_rows, weight.T, preferred_element_type=jnp.float32).astype(jnp.bfloat16)
        carry = carry.at[index].set(grads)
        parts = jnp.einsum("pnf,pnd->pfd",
                           h_rows.reshape(N_DP, N_EXPERT * CAP, FF).astype(jnp.float32),
                           dy_rows.reshape(N_DP, N_EXPERT * CAP, D).astype(jnp.float32))
        parts = lax.optimization_barrier(parts.astype(jnp.bfloat16)).astype(jnp.float32)
        return carry, jnp.sum(parts, 0)

    init = jnp.zeros((total + 1, FF), jnp.bfloat16)
    q_all, grad_down = lax.scan(per_expert, init, (table, w_down))
    qf = q_all[:total].reshape(TOKENS, TOP, FF).astype(jnp.float32)
    route_grad = jnp.sum(qf * hidden.astype(jnp.float32), -1)
    d_hidden = weights * qf
    d_gate = d_hidden * up * sig * (1.0 + gate * (1.0 - sig))
    d_up = d_hidden * act
    grad_gate_up = jnp.concatenate([d_gate, d_up], -1).astype(jnp.bfloat16)
    return grad_gate_up, route_grad, grad_down
```

```python
import functools

import jax
import jax.numpy as jnp
from jax import lax
from jax.experimental import pallas as pl
from jax.experimental.pallas import tpu as pltpu
from jax.sharding import PartitionSpec as P

BF16 = jnp.bfloat16
F32 = jnp.float32
ANY = pl.BlockSpec(memory_space=pl.ANY)
SMEM = pl.BlockSpec(memory_space=pltpu.SMEM)
LIMIT = 56 * 1024 * 1024
ROWS = 16


def call(kernel, flops, moved, **kw):
    return pl.pallas_call(
        kernel,
        compiler_params=pltpu.CompilerParams(vmem_limit_bytes=LIMIT),
        cost_estimate=pl.CostEstimate(flops=int(flops), bytes_accessed=int(moved), transcendentals=0),
        **kw,
    )


def hidden_body(nd, top, chunks, pos, gu, wt, idt, *rest):
    outs, keep, rows, packed = rest[: nd * chunks], rest[nd * chunks], rest[-2], rest[-1]
    step = pl.program_id(0)
    block, units = gu.shape[0], gu.shape[1] // 2
    g = gu[:, :units].astype(F32)
    u = gu[:, units:].astype(F32)
    h = g * jax.nn.sigmoid(g) * u
    for c in range(units // 128):
        rows[c, pl.ds(pl.multiple_of(step * block, block), block), :] = h[:, c * 128 : (c + 1) * 128]

    @pl.when(step == pl.num_programs(0) - 1)
    def _():
        tokens = wt.shape[1]
        slice_units = packed.shape[1]
        for k in range(top):
            for c in range(units // 128):
                part = rows[c, pl.ds(k, tokens, stride=top), :]
                part = part.T.astype(BF16)
                keep[c * 128 : (c + 1) * 128, k * tokens : (k + 1) * tokens] = part
        for z in range(nd):
            for k in range(top):
                w = wt[k : k + 1, :]
                part = keep[z * slice_units : (z + 1) * slice_units, k * tokens : (k + 1) * tokens]
                packed[z, :, k * tokens : (k + 1) * tokens] = (part.astype(F32) * w).astype(BF16)
        size = slice_units // chunks
        for s in range(nd):
            z = lax.rem(pos[0] + s, nd)
            for c in range(chunks):
                outs[s * chunks + c][:size, :] = packed[z, c * size : (c + 1) * size, :]
            for k in range(top):
                outs[s * chunks][size:, k * tokens : (k + 1) * tokens] = jnp.broadcast_to(
                    idt[k : k + 1, :], (ROWS, tokens)
                ).astype(BF16)


def back_body(nw, nd, top, eids, *refs):
    ws, cots, ids = refs[:nw], refs[nw : nw + nd], refs[nw + nd : nw + 2 * nd]
    outs = refs[nw + 2 * nd : nw + 3 * nd]
    wv, cv, idv, grads, sem = refs[nw + 3 * nd :]
    names = [eids[e] for e in range(eids.shape[0])]
    tokens = cots[0].shape[0]
    units = wv.shape[1]
    copies = []
    for s in range(nd):
        copies.append(pltpu.make_async_copy(cots[s], cv.at[pl.ds(s * tokens, tokens), :], sem.at[s]))
        first = ids[s].shape[0] - ROWS
        copies.append(pltpu.make_async_copy(ids[s].at[pl.ds(first, ROWS), :], idv.at[s], sem.at[nd + s]))
    at, places = 0, []
    for i, w in enumerate(ws):
        places.append((at, w.shape[0]))
        copies.append(pltpu.make_async_copy(w, wv.at[pl.ds(at, w.shape[0])], sem.at[2 * nd + i]))
        at += w.shape[0]
    for c in copies:
        c.start()
    for c in copies[: 2 * nd]:
        c.wait()
    for i, (start, n) in enumerate(places):
        copies[2 * nd + i].wait()
        w = wv[start : start + n].reshape(n * units, wv.shape[2])
        got = lax.dot_general(w, cv[...], (((1,), (1,)), ((), ())), preferred_element_type=F32)
        grads[start : start + n] = got.reshape(n, units, cv.shape[0])
    for s in range(nd):
        cols = slice(s * tokens, (s + 1) * tokens)

        def body(j, _, s=s, cols=cols):
            f = pl.multiple_of(j * ROWS, ROWS)
            held = [grads[e, pl.ds(f, ROWS), cols] for e in range(at)]
            for k in range(top):
                span = slice(k * tokens, (k + 1) * tokens)
                row = idv[s, :, span].astype(F32)
                acc = jnp.zeros((ROWS, tokens), F32)
                for e in range(at):
                    acc = jnp.where(row == names[e], held[e], acc)
                outs[s][pl.ds(f, ROWS), span] = acc.astype(BF16)
            return 0

        lax.fori_loop(0, units // ROWS, body, 0)


def down_body(nb, top, plan, columns, eids, *refs):
    cots, hs, ids = refs[:nb], refs[nb : 2 * nb], refs[2 * nb : 3 * nb]
    outs = refs[3 * nb : 3 * nb + len(plan)]
    cv, hv, idv, dense, sem = refs[3 * nb + len(plan) :]
    experts = eids.shape[0]
    tokens = cots[0].shape[0]
    units = hv.shape[1]
    copies = []
    for b in range(nb):
        first = ids[b].shape[0] - ROWS
        copies.append(pltpu.make_async_copy(hs[b].at[pl.ds(0, units), :], hv.at[b], sem.at[b]))
        copies.append(pltpu.make_async_copy(ids[b].at[pl.ds(first, ROWS), :], idv.at[b], sem.at[nb + b]))
    for b in range(nb):
        copies.append(pltpu.make_async_copy(cots[b], cv.at[pl.ds(b * tokens, tokens), :], sem.at[2 * nb + b]))
    for c in copies:
        c.start()
    names = [eids[e] for e in range(experts)]
    for b in range(nb):
        copies[2 * b].wait()
        copies[2 * b + 1].wait()
        cols = slice(b * tokens, (b + 1) * tokens)

        def body(j, _, b=b, cols=cols):
            f = pl.multiple_of(j * ROWS, ROWS)
            spans = [slice(k * tokens, (k + 1) * tokens) for k in range(top)]
            held = [hv[b, pl.ds(f, ROWS), span].astype(F32) for span in spans]
            for e in range(experts):
                acc = jnp.zeros((ROWS, tokens), F32)
                for k in range(top):
                    acc = jnp.where(idv[b, :, spans[k]].astype(F32) == names[e], held[k], acc)
                dense[e, pl.ds(f, ROWS), cols] = acc.astype(BF16)
            return 0

        lax.fori_loop(0, units // ROWS, body, 0)
    for c in copies[2 * nb :]:
        c.wait()
    width = cv.shape[1]
    lhs = dense[...].reshape(experts * units, nb * tokens)
    for start in range(0, width, columns):
        got = jnp.dot(lhs, cv[:, start : start + columns], preferred_element_type=F32)
        got = got.astype(BF16).reshape(experts, units, columns)
        for out, (groups, low, high) in zip(outs, plan):
            if low <= start < high:
                per = out.shape[1]
                for i, r in enumerate(groups):
                    out[i, :, :, start - low : start - low + columns] = got[r * per : (r + 1) * per]


def final_body(nd, top, pos, *refs):
    backs, (gu, wt, keep, out, route, turned, rows) = refs[:nd], refs[nd:]
    step = pl.program_id(0)
    block, units = gu.shape[0], gu.shape[1] // 2
    tokens = wt.shape[1]

    @pl.when(step == 0)
    def _():
        size = backs[0].shape[0]
        for k in range(top):
            span = slice(k * tokens, (k + 1) * tokens)
            w = wt[k : k + 1, :]
            total = jnp.zeros((1, tokens), F32)
            for s in range(nd):
                at = pl.multiple_of(lax.rem(pos[0] + s, nd) * size, ROWS)
                q = backs[s][:, span].astype(F32)
                total = total + jnp.sum(q * keep[pl.ds(at, size), span].astype(F32), axis=0, keepdims=True)
                turned[pl.ds(at, size), :] = q * w
            route[k : k + 1, :] = total
            for c in range(units // 128):
                rows[c, pl.ds(k, tokens, stride=top), :] = turned[c * 128 : (c + 1) * 128, :].T

    g = gu[:, :units].astype(F32)
    u = gu[:, units:].astype(F32)
    at = pl.multiple_of(step * block, block)
    d = jnp.concatenate([rows[c, pl.ds(at, block), :] for c in range(units // 128)], axis=1)
    sig = jax.nn.sigmoid(g)
    out[:, :units] = (d * u * sig * (1.0 + g * (1.0 - sig))).astype(BF16)
    out[:, units:] = (d * (g * sig)).astype(BF16)


def total_body(chunks, halves, parts, *refs):
    ins, out = refs[:-1], refs[-1]
    units = out.shape[1] // chunks
    width = out.shape[2] // halves
    at = 0
    for c in range(chunks):
        for h in range(halves):
            acc = ins[at][...].astype(F32)
            for i in range(1, parts):
                acc = acc + ins[at + i][...].astype(F32)
            at += parts
            out[:, c * units : (c + 1) * units, h * width : (h + 1) * width] = acc


def local(cotangent, saved_gate_up, route_ids, route_weights, w_down):
    tokens, top = route_ids.shape
    width = cotangent.shape[1]
    units = saved_gate_up.shape[2] // 2
    nd, ne = lax.axis_size("dp"), lax.axis_size("expert")
    per, size = w_down.shape[0], w_down.shape[1]
    routes = tokens * top
    chunks = 2 if (size // 2) % ROWS == 0 else 1
    part = size // chunks
    bits = ne.bit_length() - 1
    groups = ne // 2
    held = groups * per
    p = lax.axis_index("dp").astype(jnp.int32)
    q = lax.axis_index("expert").astype(jnp.int32)
    pos = p.reshape(1)

    def owner_of(r):
        return ((q // 2) ^ r) * 2 + q % 2

    def swap(a, mask):
        return lax.ppermute(a, "expert", [(i, i ^ mask) for i in range(ne)])

    def shift(a, s):
        return lax.ppermute(a, "dp", [(i, (i + s) % nd) for i in range(nd)])

    eids = jnp.stack([owner_of(r) * per + e for r in range(groups) for e in range(per)]).astype(F32)

    gu = saved_gate_up.reshape(routes, 2 * units)
    wt = route_weights.T
    idt = route_ids.T.astype(F32)

    cots = [cotangent] + [shift(cotangent, s) for s in range(1, nd)]
    if bits == 3:
        w_x, w_y = swap(w_down, 2), swap(w_down, 4)
        w_d = [swap(w_x[: per // 2], 4), swap(w_y[per // 2 :], 2)]
        weights = [w_down, w_x, w_y] + w_d
    else:
        weights = w_down
        for b in range(1, bits):
            weights = jnp.concatenate([weights, swap(weights, 1 << b)], 0)
        weights = [weights]

    block = routes // 8
    shapes = []
    for s in range(nd):
        for c in range(chunks):
            shapes.append(jax.ShapeDtypeStruct((part + (ROWS if c == 0 else 0), routes), BF16))
    whole = lambda shape: pl.BlockSpec(shape, lambda i: (0,) * len(shape))
    made = call(
        functools.partial(hidden_body, nd, top, chunks),
        0,
        6 * units * routes * 4,
        grid=(8,),
        in_specs=[SMEM, pl.BlockSpec((block, 2 * units), lambda i: (i, 0)), whole((top, tokens)), whole((top, tokens))],
        out_specs=[whole(o.shape) for o in shapes] + [whole((units, routes))],
        out_shape=shapes + [jax.ShapeDtypeStruct((units, routes), BF16)],
        scratch_shapes=[pltpu.VMEM((units // 128, routes, 128), F32), pltpu.VMEM((nd, size, routes), BF16)],
    )(pos, gu, wt, idt)
    keep = made[-1]
    hs = [[made[s * chunks + c] for c in range(chunks)] for s in range(nd)]
    for c in range(chunks):
        for s in range(1, nd):
            hs[s][c] = shift(hs[s][c], s)

    cots_b = [swap(a, 1) for a in cots]
    hs_b = [[None] * chunks for _ in range(nd)]
    for c in range(chunks):
        for s in range(nd):
            hs_b[s][c] = swap(hs[s][c], 1)

    def back(cots, ids):
        nw = len(weights)
        n = nd * tokens
        return call(
            functools.partial(back_body, nw, nd, top),
            2 * held * size * width * n,
            2 * (held * size * width + n * width + n * top * size),
            in_specs=[SMEM] + [ANY] * (nw + 2 * nd),
            out_specs=[pl.BlockSpec(memory_space=pltpu.VMEM)] * nd,
            out_shape=[jax.ShapeDtypeStruct((size, routes), BF16)] * nd,
            scratch_shapes=[
                pltpu.VMEM((held, size, width), BF16),
                pltpu.VMEM((n, width), BF16),
                pltpu.VMEM((nd, ROWS, routes), BF16),
                pltpu.VMEM((held, size, n), F32),
                pltpu.SemaphoreType.DMA((2 * nd + nw,)),
            ],
        )(eids, *weights, *cots, *ids)

    other = back(cots_b, [h[0] for h in hs_b])
    own = back(cots, [h[0] for h in hs])
    backs = []
    for s in range(nd):
        mine = own[s] + swap(other[s], 1)
        backs.append(mine if s == 0 else shift(mine, nd - s))

    half = width // 2
    if bits == 3:
        plan = [((1, 3), 0, half), ((0, 2), 0, half), ((2, 3), half, width), ((0, 1), half, width)]
    else:
        plan = [(tuple(range(groups)), 0, width)]
    nb = 2 * nd
    cots_all = [a for s in range(nd) for a in (cots[s], cots_b[s])]
    first = [a for s in range(nd) for a in (hs[s][0], hs_b[s][0])]
    terms = []
    for c in range(chunks):
        parts = call(
            functools.partial(down_body, nb, top, plan, 512),
            2 * held * part * width * nb * tokens,
            2 * (held * part * width + nb * tokens * width + nb * routes * part),
            in_specs=[SMEM] + [ANY] * (3 * nb),
            out_specs=[pl.BlockSpec(memory_space=pltpu.VMEM)] * len(plan),
            out_shape=[jax.ShapeDtypeStruct((len(g), per, part, b - a), BF16) for g, a, b in plan],
            scratch_shapes=[
                pltpu.VMEM((nb * tokens, width), BF16),
                pltpu.VMEM((nb, part, routes), BF16),
                pltpu.VMEM((nb, ROWS, routes), BF16),
                pltpu.VMEM((held, part, nb * tokens), BF16),
                pltpu.SemaphoreType.DMA((3 * nb,)),
            ],
        )(eids, *cots_all, *[a for s in range(nd) for a in (hs[s][c], hs_b[s][c])], *first)
        if bits == 3:
            for (send, kept), (one, two) in (((parts[0], parts[1]), (2, 4)), ((parts[2], parts[3]), (4, 2))):
                got = swap(send, one)
                mid = (kept[1].astype(F32) + got[1].astype(F32)).astype(BF16)
                terms += [kept[0], got[0], swap(mid, two)]
        else:
            acc = parts[0]
            for b in reversed(range(1, bits)):
                n = acc.shape[0] // 2
                acc = (acc[:n].astype(F32) + swap(acc[n:], 1 << b).astype(F32)).astype(BF16)
            terms.append(acc[0])
    halves, parts = (2, 3) if bits == 3 else (1, 1)
    grad_down = call(
        functools.partial(total_body, chunks, halves, parts),
        0,
        2 * 5 * per * size * width,
        out_shape=jax.ShapeDtypeStruct((per, size, width), F32),
    )(*terms)

    out, route = call(
        functools.partial(final_body, nd, top),
        0,
        8 * units * routes * 4,
        grid=(8,),
        in_specs=[SMEM]
        + [whole((size, routes))] * nd
        + [pl.BlockSpec((block, 2 * units), lambda i: (i, 0)), whole((top, tokens)), whole((units, routes))],
        out_specs=[pl.BlockSpec((block, 2 * units), lambda i: (i, 0)), whole((top, tokens))],
        out_shape=[
            jax.ShapeDtypeStruct((routes, 2 * units), BF16),
            jax.ShapeDtypeStruct((top, tokens), F32),
        ],
        scratch_shapes=[pltpu.VMEM((units, tokens), F32), pltpu.VMEM((units // 128, routes, 128), F32)],
    )(pos, *backs, gu, wt, keep)
    return out.reshape(tokens, top, 2 * units), route.T, grad_down


def solution(mesh):
    return jax.shard_map(
        local,
        mesh=mesh,
        in_specs=(
            P(("dp", "expert"), None),
            P(("dp", "expert"), None, None),
            P(("dp", "expert"), None),
            P(("dp", "expert"), None),
            P("expert", "dp", None),
        ),
        out_specs=(
            P(("dp", "expert"), None, None),
            P(("dp", "expert"), None),
            P("expert", "dp", None),
        ),
        check_vma=False,
    )
```

```python
import functools

import jax
import jax.numpy as jnp
from jax import lax
from jax.experimental import pallas as pl
from jax.experimental.pallas import tpu as pltpu
from jax.sharding import PartitionSpec as P

BF16 = jnp.bfloat16
F32 = jnp.float32
ANY = pl.BlockSpec(memory_space=pl.ANY)
VMEM = pl.BlockSpec(memory_space=pltpu.VMEM)
SMEM = pl.BlockSpec(memory_space=pltpu.SMEM)
LIMIT = 56 * 1024 * 1024
ROWS = 16


def call(kernel, flops, moved, **kw):
    return pl.pallas_call(
        kernel,
        compiler_params=pltpu.CompilerParams(vmem_limit_bytes=LIMIT),
        cost_estimate=pl.CostEstimate(flops=int(flops), bytes_accessed=int(moved), transcendentals=0),
        **kw,
    )


def hidden_body(nd, top, chunks, pos, gu, wt, *rest):
    outs, keep, rows, packed = rest[: nd * chunks], rest[nd * chunks], rest[-2], rest[-1]
    step = pl.program_id(0)
    block, units = gu.shape[0], gu.shape[1] // 2
    g = gu[:, :units].astype(F32)
    u = gu[:, units:].astype(F32)
    h = g * jax.nn.sigmoid(g) * u
    for c in range(units // 128):
        rows[c, pl.ds(pl.multiple_of(step * block, block), block), :] = h[:, c * 128 : (c + 1) * 128]

    @pl.when(step == pl.num_programs(0) - 1)
    def _():
        tokens = wt.shape[1]
        slice_units = packed.shape[1]
        for k in range(top):
            for c in range(units // 128):
                part = rows[c, pl.ds(k, tokens, stride=top), :]
                part = part.T.astype(BF16)
                keep[c * 128 : (c + 1) * 128, k * tokens : (k + 1) * tokens] = part
        for z in range(nd):
            for k in range(top):
                w = wt[k : k + 1, :]
                part = keep[z * slice_units : (z + 1) * slice_units, k * tokens : (k + 1) * tokens]
                packed[z, :, k * tokens : (k + 1) * tokens] = (part.astype(F32) * w).astype(BF16)
        size = slice_units // chunks
        for s in range(nd):
            z = lax.rem(pos[0] + s, nd)
            for c in range(chunks):
                outs[s * chunks + c][0, :size, :] = packed[z, c * size : (c + 1) * size, :]


def spread(names, idv, top):
    for b in range(idv.shape[0]):
        rows = names[b].astype(F32)
        for k in range(top):
            idv[b, k] = jnp.broadcast_to(rows[k : k + 1, :], idv.shape[2:]).astype(BF16)


def tagged(eids, tokens):
    return [jnp.full((ROWS, tokens), eids[e], F32).astype(BF16) for e in range(eids.shape[0])]


def back_body(nw, groups, top, eids, *refs):
    ws, cots, outs = refs[:nw], refs[nw : nw + groups], refs[nw + groups : nw + 2 * groups]
    wv, cv, nv, idv, grads, sem = refs[nw + 2 * groups :]
    units, width = wv.shape[1:]
    blocks, tokens = idv.shape[0], idv.shape[3]
    per = blocks // groups
    copies = []
    for g in range(groups):
        copies.append(
            pltpu.make_async_copy(
                cots[g].at[:, pl.ds(0, width)], cv.at[pl.ds(g * per * tokens, per * tokens), :], sem.at[g]
            )
        )
        for b in range(per):
            src = cots[g].at[pl.ds(b * tokens, ROWS), pl.ds(width, tokens)]
            copies.append(pltpu.make_async_copy(src, nv.at[g * per + b], sem.at[groups + g * per + b]))
    at, places = 0, []
    for i, w in enumerate(ws):
        places.append((at, w.shape[0]))
        copies.append(pltpu.make_async_copy(w, wv.at[pl.ds(at, w.shape[0])], sem.at[groups + blocks + i]))
        at += w.shape[0]
    for c in copies:
        c.start()
    for c in copies[: groups + blocks]:
        c.wait()
    spread(nv, idv, top)
    tags = tagged(eids, tokens)
    for i, (start, count) in enumerate(places):
        copies[groups + blocks + i].wait()
        w = wv[start : start + count].reshape(count * units, width)
        got = lax.dot_general(w, cv[...], (((1,), (1,)), ((), ())), preferred_element_type=F32)
        grads[start : start + count] = got.astype(BF16).reshape(count, units, cv.shape[0])
    for s in range(blocks):
        cols = slice(s * tokens, (s + 1) * tokens)

        def body(j, _, s=s, cols=cols):
            f = pl.multiple_of(j * ROWS, ROWS)
            held = [grads[e, pl.ds(f, ROWS), cols] for e in range(at)]
            for k in range(top):
                row = idv[s, k]
                acc = jnp.zeros((ROWS, tokens), BF16)
                for e in range(at):
                    acc = jnp.where(row == tags[e], held[e], acc)
                outs[s // per][s % per, pl.ds(f, ROWS), k * tokens : (k + 1) * tokens] = acc
            return 0

        lax.fori_loop(0, units // ROWS, body, 0)


def down_body(top, plan, columns, eids, *refs):
    cots, hs, outs = refs[:2], refs[2:4], refs[4 : 4 + len(plan)]
    cv, hv, nv, idv, dense, result, sem = refs[4 + len(plan) :]
    experts, units = dense.shape[:2]
    nb, tokens = idv.shape[0], idv.shape[3]
    half = nb // 2
    width = cv.shape[1]
    early, late = [], []
    for i in range(2):
        early.append(pltpu.make_async_copy(hs[i], hv.at[pl.ds(i * half, half)], sem.at[i]))
        for b in range(half):
            src = cots[i].at[pl.ds(b * tokens, ROWS), pl.ds(width, tokens)]
            early.append(pltpu.make_async_copy(src, nv.at[i * half + b], sem.at[4 + i * half + b]))
        src = cots[i].at[:, pl.ds(0, width)]
        late.append(pltpu.make_async_copy(src, cv.at[pl.ds(i * half * tokens, half * tokens), :], sem.at[2 + i]))
    for c in early:
        c.start()
    for c in early:
        c.wait()
    for c in late:
        c.start()
    spread(nv, idv, top)
    tags = tagged(eids, tokens)
    for b in range(nb):
        cols = slice(b * tokens, (b + 1) * tokens)

        def body(j, _, b=b, cols=cols):
            f = pl.multiple_of(j * ROWS, ROWS)
            held = [hv[b, pl.ds(f, ROWS), k * tokens : (k + 1) * tokens] for k in range(top)]
            rows = [idv[b, k] for k in range(top)]
            for e in range(experts):
                acc = jnp.zeros((ROWS, tokens), BF16)
                for k in range(top):
                    acc = jnp.where(rows[k] == tags[e], held[k], acc)
                dense[e, pl.ds(f, ROWS), cols] = acc
            return 0

        lax.fori_loop(0, units // ROWS, body, 0)
    for c in late:
        c.wait()
    lhs = dense[...].reshape(experts * units, nb * tokens)
    copies = []
    for t, start in enumerate(range(0, width, columns)):
        got = jnp.dot(lhs, cv[:, start : start + columns], preferred_element_type=F32)
        result[t] = got.astype(BF16).reshape(experts, units, columns)
        for out, (groups, low, high) in zip(outs, plan):
            if low <= start < high:
                per = out.shape[1]
                for i, r in enumerate(groups):
                    dst = out.at[i, :, :, pl.ds(start - low, columns)]
                    src = result.at[t, pl.ds(r * per, per)]
                    copies.append(pltpu.make_async_copy(src, dst, sem.at[4 + nb + len(copies)]))
                    copies[-1].start()
    for c in copies:
        c.wait()


def final_body(nd, top, pos, *refs):
    backs, (g_ref, u_ref, wt, keep, out, route, turned, rows, held, sem) = refs[:nd], refs[nd:]
    step = pl.program_id(0)
    last = pl.num_programs(0) - 1
    tokens = wt.shape[1]
    units = turned.shape[0]

    @pl.when(step == 0)
    def _():
        size = backs[0].shape[0]
        for s in range(nd):
            at = pl.multiple_of(lax.rem(pos[0] + s, nd) * size, ROWS)
            turned[pl.ds(at, size), :] = backs[s][...]
        route[...] = jnp.zeros_like(route)

    f = pl.multiple_of(step * 128, 128)

    def copies(n):
        slot = lax.rem(n, 2)
        for i in range(2):
            col = pl.multiple_of(i * units + n * 128, 128)
            yield pltpu.make_async_copy(held.at[slot, i], out.at[:, pl.ds(col, 128)], sem.at[slot, i])

    for k in range(top):
        span = slice(k * tokens, (k + 1) * tokens)
        q = turned[pl.ds(f, 128), span].astype(F32)
        route[k : k + 1, :] += jnp.sum(q * keep[:, span].astype(F32), axis=0, keepdims=True)
        rows[pl.ds(k, tokens, stride=top), :] = (q * wt[k : k + 1, :]).T

    @pl.when(step >= 2)
    def _():
        for c in copies(step - 2):
            c.wait()

    slot = lax.rem(step, 2)
    g = g_ref[...].astype(F32)
    u = u_ref[...].astype(F32)
    d = rows[...]
    sig = jax.nn.sigmoid(g)
    held[slot, 0] = (d * u * sig * (1.0 + g * (1.0 - sig))).astype(BF16)
    held[slot, 1] = (d * (g * sig)).astype(BF16)
    for c in copies(step):
        c.start()

    @pl.when(step == last)
    def _():
        for n in (last - 1, last):
            for c in copies(n):
                c.wait()


def total_body(chunks, halves, parts, *refs):
    ins, out = refs[:-1], refs[-1]
    width = out.shape[3] // halves
    at = 0
    for c in range(chunks):
        for h in range(halves):
            acc = ins[at][0].astype(F32)
            for i in range(1, parts):
                acc = acc + ins[at + i][0].astype(F32)
            at += parts
            out[:, c, :, h * width : (h + 1) * width] = acc


def local(cotangent, saved_gate_up, route_ids, route_weights, w_down):
    tokens, top = route_ids.shape
    width = cotangent.shape[1]
    units = saved_gate_up.shape[2] // 2
    nd, ne = lax.axis_size("dp"), lax.axis_size("expert")
    per, size = w_down.shape[0], w_down.shape[1]
    routes = tokens * top
    chunks = 2 if (size // 2) % ROWS == 0 else 1
    part = size // chunks
    bits = ne.bit_length() - 1
    groups = ne // 2
    held = groups * per
    p = lax.axis_index("dp").astype(jnp.int32)
    q = lax.axis_index("expert").astype(jnp.int32)
    pos = p.reshape(1)

    def owner_of(r):
        return ((q // 2) ^ r) * 2 + q % 2

    def swap(a, mask):
        return lax.ppermute(a, "expert", [(i, i ^ mask) for i in range(ne)])

    def shift(a, s):
        return lax.ppermute(a, "dp", [(i, (i + s) % nd) for i in range(nd)])

    eids = jnp.stack([owner_of(r) * per + e for r in range(groups) for e in range(per)]).astype(F32)

    gu = saved_gate_up.reshape(routes, 2 * units)
    wt = route_weights.T

    names = jnp.zeros((tokens, 128 * -(-tokens // 128)), BF16).at[:top, :tokens].set(route_ids.T.astype(BF16))
    sent = jnp.concatenate([cotangent, names], 1)

    def after(a, *done):
        return lax.optimization_barrier((a,) + done)[0]

    block = routes // 8
    shapes = []
    for s in range(nd):
        for c in range(chunks):
            shapes.append(jax.ShapeDtypeStruct((1, part, routes), BF16))
    whole = lambda shape: pl.BlockSpec(shape, lambda i: (0,) * len(shape))
    made = call(
        functools.partial(hidden_body, nd, top, chunks),
        0,
        6 * units * routes * 4,
        grid=(8,),
        in_specs=[SMEM, pl.BlockSpec((block, 2 * units), lambda i: (i, 0)), whole((top, tokens))],
        out_specs=[whole(o.shape) for o in shapes] + [whole((units, routes))],
        out_shape=shapes + [jax.ShapeDtypeStruct((units, routes), BF16)],
        scratch_shapes=[pltpu.VMEM((units // 128, routes, 128), F32), pltpu.VMEM((nd, size, routes), BF16)],
    )(pos, gu, wt)
    keep = made[-1]
    hs = [[made[s * chunks + c] for s in range(nd)] for c in range(chunks)]

    near = [swap(w_down, 2), swap(w_down, 4)] if bits == 3 else []
    far = [shift(sent, s) for s in range(1, nd)]
    near, far, hs, keep, sent = lax.optimization_barrier((near, far, hs, keep, sent))

    if bits == 3:
        corner = [swap(near[0][: per // 2], 4), swap(near[1][per // 2 :], 2)]
        weights = [w_down] + near + corner
    else:
        weights = w_down
        for b in range(1, bits):
            weights = jnp.concatenate([weights, swap(weights, 1 << b)], 0)
        weights = [weights]
    cots = jnp.concatenate([sent] + far, 0)

    def send(c):
        return [hs[c][0]] + [shift(hs[c][s], s) for s in range(1, nd)]

    mine = [send(0)]
    weights, cots, mine, hs = lax.optimization_barrier((weights, cots, mine, hs))

    cots_theirs = swap(cots, 1)
    mine[0] = jnp.concatenate(mine[0], 0)
    theirs = [swap(mine[0], 1)]
    for c in range(1, chunks):
        mine.append(send(c))

    def back(eids, *cots):
        nw, ng = len(weights), len(cots)
        n = ng * nd * tokens
        return call(
            functools.partial(back_body, nw, ng, top),
            2 * held * size * width * n,
            2 * (held * size * width + n * width + n * top * size),
            in_specs=[SMEM] + [ANY] * (nw + ng),
            out_specs=[VMEM] * ng,
            out_shape=[jax.ShapeDtypeStruct((nd, size, routes), BF16)] * ng,
            scratch_shapes=[
                pltpu.VMEM((held, size, width), BF16),
                pltpu.VMEM((n, width), BF16),
                pltpu.VMEM((ng * nd, ROWS, tokens), BF16),
                pltpu.VMEM((ng * nd, top, ROWS, tokens), BF16),
                pltpu.VMEM((held, size, n), BF16),
                pltpu.SemaphoreType.DMA((nw + ng + ng * nd,)),
            ],
        )(eids, *weights, *cots)

    half = width // 2
    if bits == 3:
        plan = [((1, 3), 0, half), ((0, 2), 0, half), ((2, 3), half, width), ((0, 1), half, width)]
    else:
        plan = [(tuple(range(groups)), 0, width)]
    nb = 2 * nd
    columns = 512

    def down(eids, c):
        return call(
            functools.partial(down_body, top, plan, columns),
            2 * held * part * width * nb * tokens,
            2 * (held * part * width + nb * tokens * width + nb * routes * part),
            in_specs=[SMEM] + [ANY] * 4,
            out_specs=[ANY] * len(plan),
            out_shape=[jax.ShapeDtypeStruct((len(g), per, part, b - a), BF16) for g, a, b in plan],
            scratch_shapes=[
                pltpu.VMEM((nb * tokens, width), BF16),
                pltpu.VMEM((nb, part, routes), BF16),
                pltpu.VMEM((nb, ROWS, tokens), BF16),
                pltpu.VMEM((nb, top, ROWS, tokens), BF16),
                pltpu.VMEM((held, part, nb * tokens), BF16),
                pltpu.VMEM((width // columns, held, part, columns), BF16),
                pltpu.SemaphoreType.DMA((4 + nb + width // columns * groups,)),
            ],
        )(eids, cots, cots_theirs, mine[c], theirs[c])

    sums = [down(eids, 0)]
    weights, cots, cots_theirs, mine, theirs, sums = lax.optimization_barrier(
        (weights, cots, cots_theirs, mine, theirs, sums)
    )

    def first_step(parts):
        return [swap(parts[0], 2), swap(parts[2], 4)] if bits == 3 else []

    got = [first_step(sums[0])]
    for c in range(1, chunks):
        mine[c] = jnp.concatenate(mine[c], 0)
        theirs.append(swap(mine[c], 1))
    own, other = back(eids, cots, cots_theirs)
    cots, cots_theirs, mine, theirs, sums, got, own, other = lax.optimization_barrier(
        (cots, cots_theirs, mine, theirs, sums, got, own, other)
    )

    def second_step(parts, got):
        mids = [(parts[i][1:].astype(F32) + a[1:].astype(F32)).astype(BF16) for i, a in zip((1, 3), got)]
        return [swap(mids[0], 4), swap(mids[1], 2)]

    ends = [second_step(sums[0], got[0])] if bits == 3 else []
    other = swap(other, 1)
    for c in range(1, chunks):
        sums.append(down(eids, c))
    sums, got, ends, own, other = lax.optimization_barrier((sums, got, ends, own, other))

    for c in range(1, chunks):
        got.append(first_step(sums[c]))
    backs = [own[s] + other[s] for s in range(nd)]
    backs = [backs[0]] + [shift(backs[s], nd - s) for s in range(1, nd)]
    sums, got, backs = lax.optimization_barrier((sums, got, backs))

    terms = []
    if bits == 3:
        for c in range(chunks):
            if c:
                ends.append(second_step(sums[c], got[c]))
            for i in range(2):
                terms += [sums[c][2 * i + 1], got[c][i], ends[c][i]]
    else:
        for parts in sums:
            acc = parts[0]
            for b in reversed(range(1, bits)):
                n = acc.shape[0] // 2
                acc = (acc[:n].astype(F32) + swap(acc[n:], 1 << b).astype(F32)).astype(BF16)
            terms.append(acc)
    halves, parts = (2, 3) if bits == 3 else (1, 1)
    rows = part // 2 if part % (2 * ROWS) == 0 else part
    first = pl.BlockSpec((1, per, rows, width // halves), lambda j: (0, 0, j, 0))
    grad_down = call(
        functools.partial(total_body, chunks, halves, parts),
        0,
        2 * 5 * per * size * width,
        grid=(part // rows,),
        in_specs=[first] * len(terms),
        out_specs=pl.BlockSpec((per, chunks, rows, width), lambda j: (0, 0, j, 0)),
        out_shape=jax.ShapeDtypeStruct((per, chunks, part, width), F32),
    )(*terms).reshape(per, size, width)

    cols = units // 128
    out, route = call(
        functools.partial(final_body, nd, top),
        0,
        8 * units * routes * 4,
        grid=(cols,),
        in_specs=[SMEM]
        + [whole((size, routes))] * nd
        + [
            pl.BlockSpec((routes, 128), lambda i: (0, i)),
            pl.BlockSpec((routes, 128), lambda i: (0, cols + i)),
            whole((top, tokens)),
            pl.BlockSpec((128, routes), lambda i: (i, 0)),
        ],
        out_specs=[ANY, whole((top, tokens))],
        out_shape=[
            jax.ShapeDtypeStruct((routes, 2 * units), BF16),
            jax.ShapeDtypeStruct((top, tokens), F32),
        ],
        scratch_shapes=[
            pltpu.VMEM((units, routes), BF16),
            pltpu.VMEM((routes, 128), F32),
            pltpu.VMEM((2, 2, routes, 128), BF16),
            pltpu.SemaphoreType.DMA((2, 2)),
        ],
    )(pos, *backs, gu, gu, wt, keep)
    return out.reshape(tokens, top, 2 * units), route.T, grad_down


def solution(mesh):
    return jax.shard_map(
        local,
        mesh=mesh,
        in_specs=(
            P(("dp", "expert"), None),
            P(("dp", "expert"), None, None),
            P(("dp", "expert"), None),
            P(("dp", "expert"), None),
            P("expert", "dp", None),
        ),
        out_specs=(
            P(("dp", "expert"), None, None),
            P(("dp", "expert"), None),
            P("expert", "dp", None),
        ),
        check_vma=False,
    )
```

```python
import functools

import jax
import jax.numpy as jnp
from jax import lax
from jax.experimental import pallas as pl
from jax.experimental.pallas import tpu as pltpu
from jax.sharding import PartitionSpec as P

BF16 = jnp.bfloat16
F32 = jnp.float32
ANY = pl.BlockSpec(memory_space=pl.ANY)
VMEM = pl.BlockSpec(memory_space=pltpu.VMEM)
SMEM = pl.BlockSpec(memory_space=pltpu.SMEM)
LIMIT = 56 * 1024 * 1024
ROWS = 16


def call(kernel, flops, moved, **kw):
    return pl.pallas_call(
        kernel,
        compiler_params=pltpu.CompilerParams(vmem_limit_bytes=LIMIT),
        cost_estimate=pl.CostEstimate(flops=int(flops), bytes_accessed=int(moved), transcendentals=0),
        **kw,
    )


def hidden_body(nd, top, chunks, pos, gu, wt, *rest):
    outs, keep, rows, packed = rest[: nd * chunks], rest[nd * chunks], rest[-2], rest[-1]
    step = pl.program_id(0)
    block, units = gu.shape[0], gu.shape[1] // 2
    g = gu[:, :units].astype(F32)
    u = gu[:, units:].astype(F32)
    h = g * jax.nn.sigmoid(g) * u
    for c in range(units // 128):
        rows[c, pl.ds(pl.multiple_of(step * block, block), block), :] = h[:, c * 128 : (c + 1) * 128]

    @pl.when(step == pl.num_programs(0) - 1)
    def _():
        tokens = wt.shape[1]
        slice_units = packed.shape[1]
        for k in range(top):
            for c in range(units // 128):
                part = rows[c, pl.ds(k, tokens, stride=top), :]
                part = part.T.astype(BF16)
                keep[c * 128 : (c + 1) * 128, k * tokens : (k + 1) * tokens] = part
        for z in range(nd):
            for k in range(top):
                w = wt[k : k + 1, :]
                part = keep[z * slice_units : (z + 1) * slice_units, k * tokens : (k + 1) * tokens]
                packed[z, :, k * tokens : (k + 1) * tokens] = (part.astype(F32) * w).astype(BF16)
        size = slice_units // chunks
        for s in range(nd):
            z = lax.rem(pos[0] + s, nd)
            for c in range(chunks):
                outs[s * chunks + c][0, :size, :] = packed[z, c * size : (c + 1) * size, :]


def spread(names, idv, top):
    for b in range(idv.shape[0]):
        rows = names[b].astype(F32)
        for k in range(top):
            idv[b, k] = jnp.broadcast_to(rows[k : k + 1, :], idv.shape[2:]).astype(BF16)


def tagged(eids, tokens):
    return [jnp.full((ROWS, tokens), eids[e], F32).astype(BF16) for e in range(eids.shape[0])]


def back_body(nw, groups, top, eids, *refs):
    ng = len(groups)
    ws, cots, refs = refs[:nw], refs[nw : nw + ng], refs[nw + ng :]
    earlier = sum(begun for _, begun in groups)
    befores, outs = refs[:earlier], refs[earlier : earlier + ng]
    wv, cv, nv, idv, grads, pv, sem = refs[earlier + ng :]
    units, width = wv.shape[1:]
    blocks, tokens = idv.shape[0], idv.shape[3]
    per = blocks // ng
    ready, copies = [], []
    for g in range(ng):
        rows = pl.ds(g * per * tokens, per * tokens)
        ready.append(pltpu.make_async_copy(cots[g].at[:, pl.ds(0, width)], cv.at[rows, :], sem.at[g]))
        for b in range(per):
            src = cots[g].at[pl.ds(b * tokens, ROWS), pl.ds(width, tokens)]
            ready.append(pltpu.make_async_copy(src, nv.at[g * per + b], sem.at[ng + g * per + b]))
    at, places = 0, []
    for i, w in enumerate(ws):
        places.append((at, w.shape[0]))
        copies.append(pltpu.make_async_copy(w, wv.at[pl.ds(at, w.shape[0])], sem.at[ng + blocks + i]))
        at += w.shape[0]
    for i in range(earlier):
        copies.append(pltpu.make_async_copy(befores[i], pv.at[i], sem.at[ng + blocks + nw + i]))
    for c in ready + copies:
        c.start()
    for c in ready:
        c.wait()
    spread(nv, idv, top)
    tags = tagged(eids, tokens)
    for i, (start, count) in enumerate(places):
        copies[i].wait()
        meets = [g for g in range(ng) if groups[g][0] <= i]
        low, high = meets[0] * per * tokens, (meets[-1] + 1) * per * tokens
        w = wv[start : start + count].reshape(count * units, width)
        got = lax.dot_general(w, cv[low:high, :], (((1,), (1,)), ((), ())), preferred_element_type=F32)
        grads[start : start + count, :, low:high] = got.astype(BF16).reshape(count, units, high - low)
    for c in copies[nw:]:
        c.wait()
    source = 0
    for g, (first, begun) in enumerate(groups):
        for s in range(per):
            block = g * per + s
            cols = slice(block * tokens, (block + 1) * tokens)

            def body(j, _, g=g, s=s, block=block, cols=cols, begin=places[first][0], begun=begun, source=source):
                f = pl.multiple_of(j * ROWS, ROWS)
                held = {e: grads[e, pl.ds(f, ROWS), cols] for e in range(begin, at)}
                for k in range(top):
                    span = slice(k * tokens, (k + 1) * tokens)
                    row = idv[block, k]
                    acc = pv[source, s, pl.ds(f, ROWS), span] if begun else jnp.zeros((ROWS, tokens), BF16)
                    for e in held:
                        acc = jnp.where(row == tags[e], held[e], acc)
                    outs[g][s, pl.ds(f, ROWS), span] = acc
                return 0

            lax.fori_loop(0, units // ROWS, body, 0)
        source += begun


def down_body(top, plan, columns, eids, *refs):
    cots, hs, outs = refs[:2], refs[2:4], refs[4 : 4 + len(plan)]
    cv, hv, nv, idv, dense, result, sem = refs[4 + len(plan) :]
    experts, units = dense.shape[:2]
    nb, tokens = idv.shape[0], idv.shape[3]
    half = nb // 2
    width = cv.shape[1]
    early, late = [], []
    for i in range(2):
        early.append(pltpu.make_async_copy(hs[i], hv.at[pl.ds(i * half, half)], sem.at[i]))
        for b in range(half):
            src = cots[i].at[pl.ds(b * tokens, ROWS), pl.ds(width, tokens)]
            early.append(pltpu.make_async_copy(src, nv.at[i * half + b], sem.at[4 + i * half + b]))
        src = cots[i].at[:, pl.ds(0, width)]
        late.append(pltpu.make_async_copy(src, cv.at[pl.ds(i * half * tokens, half * tokens), :], sem.at[2 + i]))
    for c in early:
        c.start()
    for c in early:
        c.wait()
    for c in late:
        c.start()
    spread(nv, idv, top)
    tags = tagged(eids, tokens)
    for b in range(nb):
        cols = slice(b * tokens, (b + 1) * tokens)

        def body(j, _, b=b, cols=cols):
            f = pl.multiple_of(j * ROWS, ROWS)
            held = [hv[b, pl.ds(f, ROWS), k * tokens : (k + 1) * tokens] for k in range(top)]
            rows = [idv[b, k] for k in range(top)]
            for e in range(experts):
                acc = jnp.zeros((ROWS, tokens), BF16)
                for k in range(top):
                    acc = jnp.where(rows[k] == tags[e], held[k], acc)
                dense[e, pl.ds(f, ROWS), cols] = acc
            return 0

        lax.fori_loop(0, units // ROWS, body, 0)
    for c in late:
        c.wait()
    lhs = dense[...].reshape(experts * units, nb * tokens)
    copies = []
    for t, start in enumerate(range(0, width, columns)):
        got = jnp.dot(lhs, cv[:, start : start + columns], preferred_element_type=F32)
        result[t] = got.astype(BF16).reshape(experts, units, columns)
        for out, (groups, low, high) in zip(outs, plan):
            if low <= start < high:
                per = out.shape[1]
                for i, r in enumerate(groups):
                    dst = out.at[i, :, :, pl.ds(start - low, columns)]
                    src = result.at[t, pl.ds(r * per, per)]
                    copies.append(pltpu.make_async_copy(src, dst, sem.at[4 + nb + len(copies)]))
                    copies[-1].start()
    for c in copies:
        c.wait()


def final_body(nd, top, pos, *refs):
    backs, (g_ref, u_ref, wt, keep, out, route, turned, rows, held, sem) = refs[:nd], refs[nd:]
    step = pl.program_id(0)
    last = pl.num_programs(0) - 1
    tokens = wt.shape[1]
    units = turned.shape[0]

    @pl.when(step == 0)
    def _():
        size = backs[0].shape[0]
        for s in range(nd):
            at = pl.multiple_of(lax.rem(pos[0] + s, nd) * size, ROWS)
            turned[pl.ds(at, size), :] = backs[s][...]
        route[...] = jnp.zeros_like(route)

    f = pl.multiple_of(step * 128, 128)

    def copies(n):
        slot = lax.rem(n, 2)
        for i in range(2):
            col = pl.multiple_of(i * units + n * 128, 128)
            yield pltpu.make_async_copy(held.at[slot, i], out.at[:, pl.ds(col, 128)], sem.at[slot, i])

    for k in range(top):
        span = slice(k * tokens, (k + 1) * tokens)
        q = turned[pl.ds(f, 128), span].astype(F32)
        route[k : k + 1, :] += jnp.sum(q * keep[:, span].astype(F32), axis=0, keepdims=True)
        rows[pl.ds(k, tokens, stride=top), :] = (q * wt[k : k + 1, :]).T

    @pl.when(step >= 2)
    def _():
        for c in copies(step - 2):
            c.wait()

    slot = lax.rem(step, 2)
    g = g_ref[...].astype(F32)
    u = u_ref[...].astype(F32)
    d = rows[...]
    sig = jax.nn.sigmoid(g)
    held[slot, 0] = (d * u * sig * (1.0 + g * (1.0 - sig))).astype(BF16)
    held[slot, 1] = (d * (g * sig)).astype(BF16)
    for c in copies(step):
        c.start()

    @pl.when(step == last)
    def _():
        for n in (last - 1, last):
            for c in copies(n):
                c.wait()


def total_body(chunks, halves, parts, *refs):
    ins, out = refs[:-1], refs[-1]
    width = out.shape[3] // halves
    at = 0
    for c in range(chunks):
        for h in range(halves):
            acc = ins[at][0].astype(F32)
            for i in range(1, parts):
                acc = acc + ins[at + i][0].astype(F32)
            at += parts
            out[:, c, :, h * width : (h + 1) * width] = acc


def local(cotangent, saved_gate_up, route_ids, route_weights, w_down):
    tokens, top = route_ids.shape
    width = cotangent.shape[1]
    units = saved_gate_up.shape[2] // 2
    nd, ne = lax.axis_size("dp"), lax.axis_size("expert")
    per, size = w_down.shape[0], w_down.shape[1]
    routes = tokens * top
    chunks = 2 if (size // 2) % ROWS == 0 else 1
    part = size // chunks
    bits = ne.bit_length() - 1
    groups = ne // 2
    held = groups * per
    p = lax.axis_index("dp").astype(jnp.int32)
    q = lax.axis_index("expert").astype(jnp.int32)
    pos = p.reshape(1)

    def owner_of(r):
        return ((q // 2) ^ r) * 2 + q % 2

    def swap(a, mask):
        return lax.ppermute(a, "expert", [(i, i ^ mask) for i in range(ne)])

    def shift(a, s):
        return lax.ppermute(a, "dp", [(i, (i + s) % nd) for i in range(nd)])

    eids = jnp.stack([owner_of(r) * per + e for r in range(groups) for e in range(per)]).astype(F32)

    gu = saved_gate_up.reshape(routes, 2 * units)
    wt = route_weights.T

    names = jnp.zeros((tokens, 128 * -(-tokens // 128)), BF16).at[:top, :tokens].set(route_ids.T.astype(BF16))
    sent = jnp.concatenate([cotangent, names], 1)

    def after(a, *done):
        return lax.optimization_barrier((a,) + done)[0]

    block = routes // 8
    shapes = []
    for s in range(nd):
        for c in range(chunks):
            shapes.append(jax.ShapeDtypeStruct((1, part, routes), BF16))
    whole = lambda shape: pl.BlockSpec(shape, lambda i: (0,) * len(shape))
    made = call(
        functools.partial(hidden_body, nd, top, chunks),
        0,
        6 * units * routes * 4,
        grid=(8,),
        in_specs=[SMEM, pl.BlockSpec((block, 2 * units), lambda i: (i, 0)), whole((top, tokens))],
        out_specs=[whole(o.shape) for o in shapes] + [whole((units, routes))],
        out_shape=shapes + [jax.ShapeDtypeStruct((units, routes), BF16)],
        scratch_shapes=[pltpu.VMEM((units // 128, routes, 128), F32), pltpu.VMEM((nd, size, routes), BF16)],
    )(pos, gu, wt)
    keep = made[-1]
    hs = [[made[s * chunks + c] for s in range(nd)] for c in range(chunks)]

    def back(weights, groups, cots, befores):
        nw, ng, count = len(weights), len(cots), sum(w.shape[0] for w in weights)
        n = ng * nd * tokens
        return call(
            functools.partial(back_body, nw, groups, top),
            2 * count * size * width * n,
            2 * (count * size * width + n * width + n * top * size),
            in_specs=[SMEM] + [ANY] * (nw + ng + len(befores)),
            out_specs=[VMEM] * ng,
            out_shape=[jax.ShapeDtypeStruct((nd, size, routes), BF16)] * ng,
            scratch_shapes=[
                pltpu.VMEM((count, size, width), BF16),
                pltpu.VMEM((n, width), BF16),
                pltpu.VMEM((ng * nd, ROWS, tokens), BF16),
                pltpu.VMEM((ng * nd, top, ROWS, tokens), BF16),
                pltpu.VMEM((count, size, n), BF16),
                pltpu.VMEM((max(1, len(befores)), nd, size, routes), BF16),
                pltpu.SemaphoreType.DMA((nw + ng + ng * nd + len(befores),)),
            ],
        )(eids[:count], *weights, *cots, *befores)

    first = after(w_down, sent)
    near = [swap(first, 2), swap(first, 4)] if bits == 3 else []
    far = [shift(sent, s) for s in range(1, nd)]
    near, far, hs, keep, sent = lax.optimization_barrier((near, far, hs, keep, sent))

    if bits == 3:
        corner = [swap(near[0][: per // 2], 4), swap(near[1][per // 2 :], 2)]
        weights = [w_down] + near + corner
    else:
        weights = w_down
        for b in range(1, bits):
            weights = jnp.concatenate([weights, swap(weights, 1 << b)], 0)
        weights = [weights]
    cots = jnp.concatenate([sent] + far, 0)

    def send(c):
        return [hs[c][0]] + [shift(hs[c][s], s) for s in range(1, nd)]

    mine = [send(0)]
    begun = back(weights[:3], ((0, False),), [cots], []) if bits == 3 else []
    weights, cots, mine, hs, begun = lax.optimization_barrier((weights, cots, mine, hs, begun))

    half = width // 2
    if bits == 3:
        plan = [((1, 3), 0, half), ((0, 2), 0, half), ((2, 3), half, width), ((0, 1), half, width)]
    else:
        plan = [(tuple(range(groups)), 0, width)]
    nb = 2 * nd
    columns = 512

    def down(eids, c):
        return call(
            functools.partial(down_body, top, plan, columns),
            2 * held * part * width * nb * tokens,
            2 * (held * part * width + nb * tokens * width + nb * routes * part),
            in_specs=[SMEM] + [ANY] * 4,
            out_specs=[ANY] * len(plan),
            out_shape=[jax.ShapeDtypeStruct((len(g), per, part, b - a), BF16) for g, a, b in plan],
            scratch_shapes=[
                pltpu.VMEM((nb * tokens, width), BF16),
                pltpu.VMEM((nb, part, routes), BF16),
                pltpu.VMEM((nb, ROWS, tokens), BF16),
                pltpu.VMEM((nb, top, ROWS, tokens), BF16),
                pltpu.VMEM((held, part, nb * tokens), BF16),
                pltpu.VMEM((width // columns, held, part, columns), BF16),
                pltpu.SemaphoreType.DMA((4 + nb + width // columns * groups,)),
            ],
        )(eids, cots, cots_theirs, mine[c], theirs[c])

    cots_theirs = swap(cots, 1)
    mine[0] = jnp.concatenate(mine[0], 0)
    theirs = [swap(mine[0], 1)]
    for c in range(1, chunks):
        mine.append(send(c))
    groups_met = ((3 if bits == 3 else 0, bits == 3), (0, False))
    own, other = back(weights, groups_met, [cots, cots_theirs], begun)
    cots, cots_theirs, mine, theirs, own, other = lax.optimization_barrier(
        (cots, cots_theirs, mine, theirs, own, other)
    )

    other = swap(other, 1)
    for c in range(1, chunks):
        mine[c] = jnp.concatenate(mine[c], 0)
        theirs.append(swap(mine[c], 1))
    sums = [down(eids, 0)]
    cots, cots_theirs, mine, theirs, own, other, sums = lax.optimization_barrier(
        (cots, cots_theirs, mine, theirs, own, other, sums)
    )

    def first_step(parts):
        return [swap(parts[0], 2), swap(parts[2], 4)] if bits == 3 else []

    def second_step(parts, got):
        mids = [(parts[i][1:].astype(F32) + a[1:].astype(F32)).astype(BF16) for i, a in zip((1, 3), got)]
        return [swap(mids[0], 4), swap(mids[1], 2)]

    got = [first_step(sums[0])]
    backs = [own[s] + other[s] for s in range(nd)]
    backs = [a if s in (0, nd // 2) else shift(a, nd - s) for s, a in enumerate(backs)]
    for c in range(1, chunks):
        sums.append(down(eids, c))
    sums, got, backs = lax.optimization_barrier((sums, got, backs))

    backs[nd // 2] = shift(backs[nd // 2], nd - nd // 2)
    for c in range(1, chunks):
        got.append(first_step(sums[c]))
    ends = [second_step(sums[0], got[0])] if bits == 3 else []
    sums, got, backs, ends = lax.optimization_barrier((sums, got, backs, ends))

    terms = []
    if bits == 3:
        for c in range(chunks):
            if c:
                ends.append(second_step(sums[c], got[c]))
            for i in range(2):
                terms += [sums[c][2 * i + 1], got[c][i], ends[c][i]]
    else:
        for parts in sums:
            acc = parts[0]
            for b in reversed(range(1, bits)):
                n = acc.shape[0] // 2
                acc = (acc[:n].astype(F32) + swap(acc[n:], 1 << b).astype(F32)).astype(BF16)
            terms.append(acc)
    halves, parts = (2, 3) if bits == 3 else (1, 1)
    rows = part // 2 if part % (2 * ROWS) == 0 else part
    first = pl.BlockSpec((1, per, rows, width // halves), lambda j: (0, 0, j, 0))
    grad_down = call(
        functools.partial(total_body, chunks, halves, parts),
        0,
        2 * 5 * per * size * width,
        grid=(part // rows,),
        in_specs=[first] * len(terms),
        out_specs=pl.BlockSpec((per, chunks, rows, width), lambda j: (0, 0, j, 0)),
        out_shape=jax.ShapeDtypeStruct((per, chunks, part, width), F32),
    )(*terms).reshape(per, size, width)

    cols = units // 128
    out, route = call(
        functools.partial(final_body, nd, top),
        0,
        8 * units * routes * 4,
        grid=(cols,),
        in_specs=[SMEM]
        + [whole((size, routes))] * nd
        + [
            pl.BlockSpec((routes, 128), lambda i: (0, i)),
            pl.BlockSpec((routes, 128), lambda i: (0, cols + i)),
            whole((top, tokens)),
            pl.BlockSpec((128, routes), lambda i: (i, 0)),
        ],
        out_specs=[ANY, whole((top, tokens))],
        out_shape=[
            jax.ShapeDtypeStruct((routes, 2 * units), BF16),
            jax.ShapeDtypeStruct((top, tokens), F32),
        ],
        scratch_shapes=[
            pltpu.VMEM((units, routes), BF16),
            pltpu.VMEM((routes, 128), F32),
            pltpu.VMEM((2, 2, routes, 128), BF16),
            pltpu.SemaphoreType.DMA((2, 2)),
        ],
    )(pos, *backs, gu, gu, wt, keep)
    return out.reshape(tokens, top, 2 * units), route.T, grad_down


def solution(mesh):
    return jax.shard_map(
        local,
        mesh=mesh,
        in_specs=(
            P(("dp", "expert"), None),
            P(("dp", "expert"), None, None),
            P(("dp", "expert"), None),
            P(("dp", "expert"), None),
            P("expert", "dp", None),
        ),
        out_specs=(
            P(("dp", "expert"), None, None),
            P(("dp", "expert"), None),
            P("expert", "dp", None),
        ),
        check_vma=False,
    )
```

```python
import functools
import math

import jax
import jax.numpy as jnp
from jax import lax
from jax.experimental import pallas as pl
from jax.experimental.pallas import tpu as pltpu
from jax.sharding import PartitionSpec as P

BF16 = jnp.bfloat16
F32 = jnp.float32
ANY = pl.BlockSpec(memory_space=pl.ANY)
VMEM = pl.BlockSpec(memory_space=pltpu.VMEM)
SMEM = pl.BlockSpec(memory_space=pltpu.SMEM)
MIB = 1024 * 1024
ROWS = 16


def call(kernel, flops, moved, windows, **kw):
    need = windows
    for buffer in kw.get("scratch_shapes", ()):
        if jnp.issubdtype(buffer.dtype, jnp.floating):
            need += math.prod(buffer.shape) * jnp.dtype(buffer.dtype).itemsize
    return pl.pallas_call(
        kernel,
        compiler_params=pltpu.CompilerParams(vmem_limit_bytes=(26 if need < 22 * MIB else 56) * MIB),
        cost_estimate=pl.CostEstimate(flops=int(flops), bytes_accessed=int(moved), transcendentals=0),
        **kw,
    )


def hidden_body(nd, top, chunks, pos, gu, wt, *rest):
    outs, keep, rows, packed = rest[: nd * chunks], rest[nd * chunks], rest[-2], rest[-1]
    step = pl.program_id(0)
    block, units = gu.shape[0], gu.shape[1] // 2
    g = gu[:, :units].astype(F32)
    u = gu[:, units:].astype(F32)
    h = g * jax.nn.sigmoid(g) * u
    for c in range(units // 128):
        rows[c, pl.ds(pl.multiple_of(step * block, block), block), :] = h[:, c * 128 : (c + 1) * 128]

    @pl.when(step == pl.num_programs(0) - 1)
    def _():
        tokens = wt.shape[1]
        slice_units = packed.shape[1]
        for k in range(top):
            for c in range(units // 128):
                part = rows[c, pl.ds(k, tokens, stride=top), :]
                part = part.T.astype(BF16)
                keep[c * 128 : (c + 1) * 128, k * tokens : (k + 1) * tokens] = part
        for z in range(nd):
            for k in range(top):
                w = wt[k : k + 1, :]
                part = keep[z * slice_units : (z + 1) * slice_units, k * tokens : (k + 1) * tokens]
                packed[z, :, k * tokens : (k + 1) * tokens] = (part.astype(F32) * w).astype(BF16)
        size = slice_units // chunks
        for s in range(nd):
            z = lax.rem(pos[0] + s, nd)
            for c in range(chunks):
                outs[s * chunks + c][0, :size, :] = packed[z, c * size : (c + 1) * size, :]


def spread(names, idv, top):
    for b in range(idv.shape[0]):
        rows = names[b].astype(F32)
        for k in range(top):
            idv[b, k] = jnp.broadcast_to(rows[k : k + 1, :], idv.shape[2:]).astype(BF16)


def tagged(eids, tokens):
    return [jnp.full((ROWS, tokens), eids[e], F32).astype(BF16) for e in range(eids.shape[0])]


def back_body(nw, groups, top, eids, *refs):
    ng = len(groups)
    ws, cots, refs = refs[:nw], refs[nw : nw + ng], refs[nw + ng :]
    earlier = sum(begun for _, begun in groups)
    befores, outs = refs[:earlier], refs[earlier : earlier + ng]
    wv, cv, nv, idv, grads, pv, sem = refs[earlier + ng :]
    units, width = wv.shape[1:]
    blocks, tokens = idv.shape[0], idv.shape[3]
    per = blocks // ng
    ready, copies = [], []
    for g in range(ng):
        rows = pl.ds(g * per * tokens, per * tokens)
        ready.append(pltpu.make_async_copy(cots[g].at[:, pl.ds(0, width)], cv.at[rows, :], sem.at[g]))
        for b in range(per):
            src = cots[g].at[pl.ds(b * tokens, ROWS), pl.ds(width, tokens)]
            ready.append(pltpu.make_async_copy(src, nv.at[g * per + b], sem.at[ng + g * per + b]))
    at, places = 0, []
    for i, w in enumerate(ws):
        places.append((at, w.shape[0]))
        copies.append(pltpu.make_async_copy(w, wv.at[pl.ds(at, w.shape[0])], sem.at[ng + blocks + i]))
        at += w.shape[0]
    for i in range(earlier):
        copies.append(pltpu.make_async_copy(befores[i], pv.at[i], sem.at[ng + blocks + nw + i]))
    for c in ready + copies:
        c.start()
    for c in ready:
        c.wait()
    spread(nv, idv, top)
    tags = tagged(eids, tokens)
    for i, (start, count) in enumerate(places):
        copies[i].wait()
        meets = [g for g in range(ng) if groups[g][0] <= i]
        low, high = meets[0] * per * tokens, (meets[-1] + 1) * per * tokens
        w = wv[start : start + count].reshape(count * units, width)
        got = lax.dot_general(w, cv[low:high, :], (((1,), (1,)), ((), ())), preferred_element_type=F32)
        grads[start : start + count, :, low:high] = got.astype(BF16).reshape(count, units, high - low)
    for c in copies[nw:]:
        c.wait()
    source = 0
    for g, (first, begun) in enumerate(groups):
        for s in range(per):
            block = g * per + s
            cols = slice(block * tokens, (block + 1) * tokens)

            def body(j, _, g=g, s=s, block=block, cols=cols, begin=places[first][0], begun=begun, source=source):
                f = pl.multiple_of(j * ROWS, ROWS)
                held = {e: grads[e, pl.ds(f, ROWS), cols] for e in range(begin, at)}
                for k in range(top):
                    span = slice(k * tokens, (k + 1) * tokens)
                    row = idv[block, k]
                    acc = pv[source, s, pl.ds(f, ROWS), span] if begun else jnp.zeros((ROWS, tokens), BF16)
                    for e in held:
                        acc = jnp.where(row == tags[e], held[e], acc)
                    outs[g][s, pl.ds(f, ROWS), span] = acc
                return 0

            lax.fori_loop(0, units // ROWS, body, 0)
        source += begun


def down_body(top, plan, columns, eids, *refs):
    cots, hs, outs = refs[:2], refs[2:4], refs[4 : 4 + len(plan)]
    cv, hv, nv, idv, dense, result, sem = refs[4 + len(plan) :]
    experts, units = dense.shape[:2]
    nb, tokens = idv.shape[0], idv.shape[3]
    half = nb // 2
    width = cv.shape[1]
    early, late = [], []
    for i in range(2):
        early.append(pltpu.make_async_copy(hs[i], hv.at[pl.ds(i * half, half)], sem.at[i]))
        for b in range(half):
            src = cots[i].at[pl.ds(b * tokens, ROWS), pl.ds(width, tokens)]
            early.append(pltpu.make_async_copy(src, nv.at[i * half + b], sem.at[4 + i * half + b]))
        src = cots[i].at[:, pl.ds(0, width)]
        late.append(pltpu.make_async_copy(src, cv.at[pl.ds(i * half * tokens, half * tokens), :], sem.at[2 + i]))
    for c in early:
        c.start()
    for c in early:
        c.wait()
    for c in late:
        c.start()
    spread(nv, idv, top)
    tags = tagged(eids, tokens)
    for b in range(nb):
        cols = slice(b * tokens, (b + 1) * tokens)

        def body(j, _, b=b, cols=cols):
            f = pl.multiple_of(j * ROWS, ROWS)
            held = [hv[b, pl.ds(f, ROWS), k * tokens : (k + 1) * tokens] for k in range(top)]
            rows = [idv[b, k] for k in range(top)]
            for e in range(experts):
                acc = jnp.zeros((ROWS, tokens), BF16)
                for k in range(top):
                    acc = jnp.where(rows[k] == tags[e], held[k], acc)
                dense[e, pl.ds(f, ROWS), cols] = acc
            return 0

        lax.fori_loop(0, units // ROWS, body, 0)
    for c in late:
        c.wait()
    lhs = dense[...].reshape(experts * units, nb * tokens)
    copies = []
    for t, start in enumerate(range(0, width, columns)):
        got = jnp.dot(lhs, cv[:, start : start + columns], preferred_element_type=F32)
        result[t] = got.astype(BF16).reshape(experts, units, columns)
        for out, (groups, low, high) in zip(outs, plan):
            if low <= start < high:
                per = out.shape[1]
                for i, r in enumerate(groups):
                    dst = out.at[i, :, :, pl.ds(start - low, columns)]
                    src = result.at[t, pl.ds(r * per, per)]
                    copies.append(pltpu.make_async_copy(src, dst, sem.at[4 + nb + len(copies)]))
                    copies[-1].start()
    for c in copies:
        c.wait()


def final_body(nd, top, pos, *refs):
    backs, (g_ref, u_ref, wt, keep, out, route, turned, rows, held, sem) = refs[:nd], refs[nd:]
    step = pl.program_id(0)
    last = pl.num_programs(0) - 1
    tokens = wt.shape[1]
    units = turned.shape[0]

    @pl.when(step == 0)
    def _():
        size = backs[0].shape[0]
        for s in range(nd):
            at = pl.multiple_of(lax.rem(pos[0] + s, nd) * size, ROWS)
            turned[pl.ds(at, size), :] = backs[s][...]
        route[...] = jnp.zeros_like(route)

    f = pl.multiple_of(step * 128, 128)

    def copies(n):
        slot = lax.rem(n, 2)
        for i in range(2):
            col = pl.multiple_of(i * units + n * 128, 128)
            yield pltpu.make_async_copy(held.at[slot, i], out.at[:, pl.ds(col, 128)], sem.at[slot, i])

    for k in range(top):
        span = slice(k * tokens, (k + 1) * tokens)
        q = turned[pl.ds(f, 128), span].astype(F32)
        route[k : k + 1, :] += jnp.sum(q * keep[:, span].astype(F32), axis=0, keepdims=True)
        rows[pl.ds(k, tokens, stride=top), :] = (q * wt[k : k + 1, :]).T

    @pl.when(step >= 2)
    def _():
        for c in copies(step - 2):
            c.wait()

    slot = lax.rem(step, 2)
    g = g_ref[...].astype(F32)
    u = u_ref[...].astype(F32)
    d = rows[...]
    sig = jax.nn.sigmoid(g)
    held[slot, 0] = (d * u * sig * (1.0 + g * (1.0 - sig))).astype(BF16)
    held[slot, 1] = (d * (g * sig)).astype(BF16)
    for c in copies(step):
        c.start()

    @pl.when(step == last)
    def _():
        for n in (last - 1, last):
            for c in copies(n):
                c.wait()


def total_body(chunks, halves, parts, *refs):
    ins, out = refs[:-1], refs[-1]
    width = out.shape[3] // halves
    at = 0
    for c in range(chunks):
        for h in range(halves):
            acc = ins[at][0].astype(F32)
            for i in range(1, parts):
                acc = acc + ins[at + i][0].astype(F32)
            at += parts
            out[:, c, :, h * width : (h + 1) * width] = acc


def local(cotangent, saved_gate_up, route_ids, route_weights, w_down):
    tokens, top = route_ids.shape
    width = cotangent.shape[1]
    units = saved_gate_up.shape[2] // 2
    nd, ne = lax.axis_size("dp"), lax.axis_size("expert")
    per, size = w_down.shape[0], w_down.shape[1]
    routes = tokens * top
    chunks = 2 if (size // 2) % ROWS == 0 else 1
    part = size // chunks
    bits = ne.bit_length() - 1
    groups = ne // 2
    held = groups * per
    p = lax.axis_index("dp").astype(jnp.int32)
    q = lax.axis_index("expert").astype(jnp.int32)
    pos = p.reshape(1)

    def owner_of(r):
        return ((q // 2) ^ r) * 2 + q % 2

    def swap(a, mask):
        return lax.ppermute(a, "expert", [(i, i ^ mask) for i in range(ne)])

    def shift(a, s):
        return lax.ppermute(a, "dp", [(i, (i + s) % nd) for i in range(nd)])

    eids = jnp.stack([owner_of(r) * per + e for r in range(groups) for e in range(per)]).astype(F32)

    gu = saved_gate_up.reshape(routes, 2 * units)
    wt = route_weights.T

    names = jnp.zeros((tokens, 128 * -(-tokens // 128)), BF16).at[:top, :tokens].set(route_ids.T.astype(BF16))
    sent = jnp.concatenate([cotangent, names], 1)

    def after(a, *done):
        return lax.optimization_barrier((a,) + done)[0]

    block = routes // 8
    shapes = []
    for s in range(nd):
        for c in range(chunks):
            shapes.append(jax.ShapeDtypeStruct((1, part, routes), BF16))
    whole = lambda shape: pl.BlockSpec(shape, lambda i: (0,) * len(shape))
    made = call(
        functools.partial(hidden_body, nd, top, chunks),
        0,
        6 * units * routes * 4,
        2 * (4 * block * units + 4 * units * routes),
        grid=(8,),
        in_specs=[SMEM, pl.BlockSpec((block, 2 * units), lambda i: (i, 0)), whole((top, tokens))],
        out_specs=[whole(o.shape) for o in shapes] + [whole((units, routes))],
        out_shape=shapes + [jax.ShapeDtypeStruct((units, routes), BF16)],
        scratch_shapes=[pltpu.VMEM((units // 128, routes, 128), F32), pltpu.VMEM((nd, size, routes), BF16)],
    )(pos, gu, wt)
    keep = made[-1]
    hs = [[made[s * chunks + c] for s in range(nd)] for c in range(chunks)]

    def back(weights, groups, cots, befores):
        nw, ng, count = len(weights), len(cots), sum(w.shape[0] for w in weights)
        n = ng * nd * tokens
        return call(
            functools.partial(back_body, nw, groups, top),
            2 * count * size * width * n,
            2 * (count * size * width + n * width + n * top * size),
            2 * 2 * ng * nd * size * routes,
            in_specs=[SMEM] + [ANY] * (nw + ng + len(befores)),
            out_specs=[VMEM] * ng,
            out_shape=[jax.ShapeDtypeStruct((nd, size, routes), BF16)] * ng,
            scratch_shapes=[
                pltpu.VMEM((count, size, width), BF16),
                pltpu.VMEM((n, width), BF16),
                pltpu.VMEM((ng * nd, ROWS, tokens), BF16),
                pltpu.VMEM((ng * nd, top, ROWS, tokens), BF16),
                pltpu.VMEM((count, size, n), BF16),
                pltpu.VMEM((max(1, len(befores)), nd, size, routes), BF16),
                pltpu.SemaphoreType.DMA((nw + ng + ng * nd + len(befores),)),
            ],
        )(eids[:count], *weights, *cots, *befores)

    first = after(w_down, sent)
    near = [swap(first, 2), swap(first, 4)] if bits == 3 else []
    far = [shift(sent, s) for s in range(1, nd)]
    near, far, hs, keep, sent = lax.optimization_barrier((near, far, hs, keep, sent))

    if bits == 3:
        corner = [swap(near[0][: per // 2], 4), swap(near[1][per // 2 :], 2)]
        weights = [w_down] + near + corner
    else:
        weights = w_down
        for b in range(1, bits):
            weights = jnp.concatenate([weights, swap(weights, 1 << b)], 0)
        weights = [weights]
    cots = jnp.concatenate([sent] + far, 0)

    def send(c):
        return [hs[c][0]] + [shift(hs[c][s], s) for s in range(1, nd)]

    mine = [send(0)]
    begun = back(weights[:3], ((0, False),), [cots], []) if bits == 3 else []
    weights, cots, mine, hs, begun = lax.optimization_barrier((weights, cots, mine, hs, begun))

    half = width // 2
    if bits == 3:
        plan = [((1, 3), 0, half), ((0, 2), 0, half), ((2, 3), half, width), ((0, 1), half, width)]
    else:
        plan = [(tuple(range(groups)), 0, width)]
    nb = 2 * nd
    columns = 512

    def down(eids, c):
        return call(
            functools.partial(down_body, top, plan, columns),
            2 * held * part * width * nb * tokens,
            2 * (held * part * width + nb * tokens * width + nb * routes * part),
            0,
            in_specs=[SMEM] + [ANY] * 4,
            out_specs=[ANY] * len(plan),
            out_shape=[jax.ShapeDtypeStruct((len(g), per, part, b - a), BF16) for g, a, b in plan],
            scratch_shapes=[
                pltpu.VMEM((nb * tokens, width), BF16),
                pltpu.VMEM((nb, part, routes), BF16),
                pltpu.VMEM((nb, ROWS, tokens), BF16),
                pltpu.VMEM((nb, top, ROWS, tokens), BF16),
                pltpu.VMEM((held, part, nb * tokens), BF16),
                pltpu.VMEM((width // columns, held, part, columns), BF16),
                pltpu.SemaphoreType.DMA((4 + nb + width // columns * groups,)),
            ],
        )(eids, cots, cots_theirs, mine[c], theirs[c])

    cots_theirs = swap(cots, 1)
    mine[0] = jnp.concatenate(mine[0], 0)
    theirs = [swap(mine[0], 1)]
    for c in range(1, chunks):
        mine.append(send(c))
    groups_met = ((3 if bits == 3 else 0, bits == 3), (0, False))
    own, other = back(weights, groups_met, [cots, cots_theirs], begun)
    cots, cots_theirs, mine, theirs, own, other = lax.optimization_barrier(
        (cots, cots_theirs, mine, theirs, own, other)
    )

    other = swap(other, 1)
    for c in range(1, chunks):
        mine[c] = jnp.concatenate(mine[c], 0)
        theirs.append(swap(mine[c], 1))
    sums = [down(eids, 0)]
    cots, cots_theirs, mine, theirs, own, other, sums = lax.optimization_barrier(
        (cots, cots_theirs, mine, theirs, own, other, sums)
    )

    def middle(parts, got):
        return [(parts[i][1:].astype(F32) + a[1:2].astype(F32)).astype(BF16) for i, a in zip((1, 3), got)]

    plane = bits == 3
    got = [[swap(sums[0][0], 2), swap(sums[0][2], 4)]] if plane else []
    backs = [own[s] + other[s] for s in range(nd)]
    backs[1] = shift(backs[1], nd - 1)
    for c in range(1, chunks):
        sums.append(down(eids, c))
    sums, got, backs = lax.optimization_barrier((sums, got, backs))

    backs = [a if s < 2 else shift(a, nd - s) for s, a in enumerate(backs)]
    mids = []
    for c in range(1, chunks if plane else 1):
        mids = middle(sums[c - 1], got[c - 1])
        got.append(
            [
                swap(jnp.concatenate([sums[c][0], mids[1]], 0), 2),
                swap(jnp.concatenate([sums[c][2], mids[0]], 0), 4),
            ]
        )
        sums, got, backs = lax.optimization_barrier((sums, got, backs))

    terms = []
    if plane:
        mids = middle(sums[-1], got[-1])
        ends = [swap(mids[0], 4), swap(mids[1], 2)]
        for c in range(chunks):
            for i in range(2):
                end = (ends[i], 0) if c == chunks - 1 else (got[c + 1][1 - i], 2)
                terms += [(sums[c][2 * i + 1], 0), (got[c][i], 0), end]
    else:
        for parts in sums:
            acc = parts[0]
            for b in reversed(range(1, bits)):
                n = acc.shape[0] // 2
                acc = (acc[:n].astype(F32) + swap(acc[n:], 1 << b).astype(F32)).astype(BF16)
            terms.append((acc, 0))
    halves, parts = (2, 3) if bits == 3 else (1, 1)
    rows = part // 2 if part % (2 * ROWS) == 0 else part
    grad_down = call(
        functools.partial(total_body, chunks, halves, parts),
        0,
        2 * 5 * per * size * width,
        2 * per * rows * width * (2 * parts + 4) * chunks,
        grid=(part // rows,),
        in_specs=[
            pl.BlockSpec((1, per, rows, width // halves), lambda j, at=at: (at, 0, j, 0)) for _, at in terms
        ],
        out_specs=pl.BlockSpec((per, chunks, rows, width), lambda j: (0, 0, j, 0)),
        out_shape=jax.ShapeDtypeStruct((per, chunks, part, width), F32),
    )(*[a for a, _ in terms]).reshape(per, size, width)

    cols = units // 128
    out, route = call(
        functools.partial(final_body, nd, top),
        0,
        8 * units * routes * 4,
        2 * (2 * units * routes + 3 * 2 * 128 * routes),
        grid=(cols,),
        in_specs=[SMEM]
        + [whole((size, routes))] * nd
        + [
            pl.BlockSpec((routes, 128), lambda i: (0, i)),
            pl.BlockSpec((routes, 128), lambda i: (0, cols + i)),
            whole((top, tokens)),
            pl.BlockSpec((128, routes), lambda i: (i, 0)),
        ],
        out_specs=[ANY, whole((top, tokens))],
        out_shape=[
            jax.ShapeDtypeStruct((routes, 2 * units), BF16),
            jax.ShapeDtypeStruct((top, tokens), F32),
        ],
        scratch_shapes=[
            pltpu.VMEM((units, routes), BF16),
            pltpu.VMEM((routes, 128), F32),
            pltpu.VMEM((2, 2, routes, 128), BF16),
            pltpu.SemaphoreType.DMA((2, 2)),
        ],
    )(pos, *backs, gu, gu, wt, keep)
    return out.reshape(tokens, top, 2 * units), route.T, grad_down


def solution(mesh):
    return jax.shard_map(
        local,
        mesh=mesh,
        in_specs=(
            P(("dp", "expert"), None),
            P(("dp", "expert"), None, None),
            P(("dp", "expert"), None),
            P(("dp", "expert"), None),
            P("expert", "dp", None),
        ),
        out_specs=(
            P(("dp", "expert"), None, None),
            P(("dp", "expert"), None),
            P("expert", "dp", None),
        ),
        check_vma=False,
    )
```

```python
import functools
import math

import jax
import jax.numpy as jnp
from jax import lax
from jax.experimental import pallas as pl
from jax.experimental.pallas import tpu as pltpu
from jax.sharding import PartitionSpec as P

BF16 = jnp.bfloat16
F32 = jnp.float32
ANY = pl.BlockSpec(memory_space=pl.ANY)
VMEM = pl.BlockSpec(memory_space=pltpu.VMEM)
SMEM = pl.BlockSpec(memory_space=pltpu.SMEM)
MIB = 1024 * 1024
ROWS = 16


def call(kernel, flops, moved, windows, **kw):
    need = windows
    for buffer in kw.get("scratch_shapes", ()):
        if jnp.issubdtype(buffer.dtype, jnp.floating):
            need += math.prod(buffer.shape) * jnp.dtype(buffer.dtype).itemsize
    return pl.pallas_call(
        kernel,
        compiler_params=pltpu.CompilerParams(vmem_limit_bytes=(26 if need < 22 * MIB else 56) * MIB),
        cost_estimate=pl.CostEstimate(flops=int(flops), bytes_accessed=int(moved), transcendentals=0),
        **kw,
    )


def hidden_body(nd, top, chunks, pos, gu, wt, *rest):
    outs, keep, rows, packed = rest[: nd * chunks], rest[nd * chunks], rest[-2], rest[-1]
    step = pl.program_id(0)
    block, units = gu.shape[0], gu.shape[1] // 2
    g = gu[:, :units].astype(F32)
    u = gu[:, units:].astype(F32)
    h = g * jax.nn.sigmoid(g) * u
    for c in range(units // 128):
        rows[c, pl.ds(pl.multiple_of(step * block, block), block), :] = h[:, c * 128 : (c + 1) * 128]

    @pl.when(step == pl.num_programs(0) - 1)
    def _():
        tokens = wt.shape[1]
        slice_units = packed.shape[1]
        for k in range(top):
            for c in range(units // 128):
                part = rows[c, pl.ds(k, tokens, stride=top), :]
                part = part.T.astype(BF16)
                keep[c * 128 : (c + 1) * 128, k * tokens : (k + 1) * tokens] = part
        for z in range(nd):
            for k in range(top):
                w = wt[k : k + 1, :]
                part = keep[z * slice_units : (z + 1) * slice_units, k * tokens : (k + 1) * tokens]
                packed[z, :, k * tokens : (k + 1) * tokens] = (part.astype(F32) * w).astype(BF16)
        size = slice_units // chunks
        for s in range(nd):
            z = lax.rem(pos[0] + s, nd)
            for c in range(chunks):
                outs[s * chunks + c][0, :size, :] = packed[z, c * size : (c + 1) * size, :]


def spread(names, idv, top):
    for b in range(idv.shape[0]):
        rows = names[b].astype(F32)
        for k in range(top):
            idv[b, k] = jnp.broadcast_to(rows[k : k + 1, :], idv.shape[2:]).astype(BF16)


def step_of(units):
    return 2 * ROWS if units % (2 * ROWS) == 0 else ROWS


def tagged(eids, tokens, step=ROWS):
    return [jnp.full((step, tokens), eids[e], F32).astype(BF16) for e in range(eids.shape[0])]


def pack_body(counts, *refs):
    ins, outs, sem = refs[: sum(counts)], refs[sum(counts) : -1], refs[-1]
    copies = []
    for count, out in zip(counts, outs):
        at = 0
        for a in ins[len(copies) : len(copies) + count]:
            dst = out.at[pl.ds(at, a.shape[0])]
            copies.append(pltpu.make_async_copy(a, dst, sem.at[len(copies)]))
            at += a.shape[0]
    for c in copies:
        c.start()
    for c in copies:
        c.wait()


def back_body(nw, nc, ng, known, top, eids, *refs):
    ws, cots, refs = refs[:nw], refs[nw : nw + nc], refs[nw + nc :]
    befores, refs = refs[: known > 0], refs[known > 0 :]
    outs, (wv, cv, nv, idv, grads, pv, sem) = refs[:ng], refs[ng:]
    units, width = wv.shape[1:]
    blocks, tokens = idv.shape[0], idv.shape[3]
    per = blocks // ng
    done = befores[0].shape[0] if known else 0
    ready, copies, block = [], [], 0
    for i, cot in enumerate(cots):
        count = cot.shape[0] // tokens
        rows = pl.ds(block * tokens, count * tokens)
        ready.append(pltpu.make_async_copy(cot.at[:, pl.ds(0, width)], cv.at[rows, :], sem.at[i]))
        for b in range(count):
            src = cot.at[pl.ds(b * tokens, ROWS), pl.ds(width, tokens)]
            ready.append(pltpu.make_async_copy(src, nv.at[block + b], sem.at[nc + block + b]))
        block += count
    at, places = 0, []
    for i, w in enumerate(ws):
        places.append((at, w.shape[0]))
        copies.append(pltpu.make_async_copy(w, wv.at[pl.ds(at, w.shape[0])], sem.at[nc + blocks + i]))
        at += w.shape[0]
    for a in befores:
        copies.append(pltpu.make_async_copy(a, pv, sem.at[nc + blocks + nw]))
    for c in ready + copies:
        c.start()
    for c in ready:
        c.wait()
    spread(nv, idv, top)
    tags = tagged(eids, tokens)
    for i, (start, count) in enumerate(places):
        copies[i].wait()
        low = done * tokens if i < known else 0
        w = wv[start : start + count].reshape(count * units, width)
        got = lax.dot_general(w, cv[low:, :], (((1,), (1,)), ((), ())), preferred_element_type=F32)
        grads[start : start + count, :, low:] = got.astype(BF16).reshape(count, units, blocks * tokens - low)
    for c in copies[nw:]:
        c.wait()
    for block in range(blocks):
        cols = slice(block * tokens, (block + 1) * tokens)
        begun = block < done
        begin = places[known][0] if begun else 0

        def body(j, _, block=block, cols=cols, begun=begun, begin=begin):
            f = pl.multiple_of(j * ROWS, ROWS)
            held = {e: grads[e, pl.ds(f, ROWS), cols] for e in range(begin, at)}
            for k in range(top):
                span = slice(k * tokens, (k + 1) * tokens)
                row = idv[block, k]
                acc = pv[block, pl.ds(f, ROWS), span] if begun else jnp.zeros((ROWS, tokens), BF16)
                for e in held:
                    acc = jnp.where(row == tags[e], held[e], acc)
                outs[block // per][block % per, pl.ds(f, ROWS), span] = acc
            return 0

        lax.fori_loop(0, units // ROWS, body, 0)


def down_body(top, plan, columns, eids, *refs):
    cots, hs, outs = refs[:2], refs[2:4], refs[4 : 4 + len(plan)]
    cv, hv, nv, idv, dense, result, sem = refs[4 + len(plan) :]
    experts, units = dense.shape[:2]
    nb, tokens = idv.shape[0], idv.shape[3]
    half = nb // 2
    width = cv.shape[1]
    early, late = [], []
    for i in range(2):
        early.append(pltpu.make_async_copy(hs[i], hv.at[pl.ds(i * half, half)], sem.at[i]))
        for b in range(half):
            src = cots[i].at[pl.ds(b * tokens, ROWS), pl.ds(width, tokens)]
            early.append(pltpu.make_async_copy(src, nv.at[i * half + b], sem.at[4 + i * half + b]))
        src = cots[i].at[:, pl.ds(0, width)]
        late.append(pltpu.make_async_copy(src, cv.at[pl.ds(i * half * tokens, half * tokens), :], sem.at[2 + i]))
    for c in early:
        c.start()
    for c in early:
        c.wait()
    for c in late:
        c.start()
    spread(nv, idv, top)
    step = idv.shape[2]
    tags = tagged(eids, tokens, step)
    for b in range(nb):
        cols = slice(b * tokens, (b + 1) * tokens)

        def body(j, _, b=b, cols=cols):
            f = pl.multiple_of(j * step, ROWS)
            held = [hv[b, pl.ds(f, step), k * tokens : (k + 1) * tokens] for k in range(top)]
            rows = [idv[b, k] for k in range(top)]
            for e in range(experts):
                acc = jnp.zeros((step, tokens), BF16)
                for k in range(top):
                    acc = jnp.where(rows[k] == tags[e], held[k], acc)
                dense[e, pl.ds(f, step), cols] = acc
            return 0

        lax.fori_loop(0, units // step, body, 0)
    for c in late:
        c.wait()
    lhs = dense[...].reshape(experts * units, nb * tokens)
    copies = []
    for t, start in enumerate(range(0, width, columns)):
        got = jnp.dot(lhs, cv[:, start : start + columns], preferred_element_type=F32)
        result[t] = got.astype(BF16).reshape(experts, units, columns)
        for out, (groups, low, high) in zip(outs, plan):
            if low <= start < high:
                per = out.shape[1]
                for i, r in enumerate(groups):
                    dst = out.at[i, :, :, pl.ds(start - low, columns)]
                    src = result.at[t, pl.ds(r * per, per)]
                    copies.append(pltpu.make_async_copy(src, dst, sem.at[4 + nb + len(copies)]))
                    copies[-1].start()
    for c in copies:
        c.wait()


def final_body(nd, top, pos, *refs):
    backs, (g_ref, u_ref, wt, keep, out, route, turned, rows, held, sem) = refs[:nd], refs[nd:]
    step = pl.program_id(0)
    last = pl.num_programs(0) - 1
    tokens = wt.shape[1]
    units = turned.shape[0]

    @pl.when(step == 0)
    def _():
        size = backs[0].shape[0]
        for s in range(nd):
            at = pl.multiple_of(lax.rem(pos[0] + s, nd) * size, ROWS)
            turned[pl.ds(at, size), :] = backs[s][...]
        route[...] = jnp.zeros_like(route)

    f = pl.multiple_of(step * 128, 128)

    def copies(n):
        slot = lax.rem(n, 2)
        for i in range(2):
            col = pl.multiple_of(i * units + n * 128, 128)
            yield pltpu.make_async_copy(held.at[slot, i], out.at[:, pl.ds(col, 128)], sem.at[slot, i])

    for k in range(top):
        span = slice(k * tokens, (k + 1) * tokens)
        q = turned[pl.ds(f, 128), span].astype(F32)
        route[k : k + 1, :] += jnp.sum(q * keep[:, span].astype(F32), axis=0, keepdims=True)
        rows[pl.ds(k, tokens, stride=top), :] = (q * wt[k : k + 1, :]).T

    @pl.when(step >= 2)
    def _():
        for c in copies(step - 2):
            c.wait()

    slot = lax.rem(step, 2)
    g = g_ref[...].astype(F32)
    u = u_ref[...].astype(F32)
    d = rows[...]
    sig = jax.nn.sigmoid(g)
    held[slot, 0] = (d * u * sig * (1.0 + g * (1.0 - sig))).astype(BF16)
    held[slot, 1] = (d * (g * sig)).astype(BF16)
    for c in copies(step):
        c.start()

    @pl.when(step == last)
    def _():
        for n in (last - 1, last):
            for c in copies(n):
                c.wait()


def total_body(chunks, halves, parts, *refs):
    ins, out = refs[:-1], refs[-1]
    width = out.shape[3] // halves
    at = 0
    for c in range(chunks):
        for h in range(halves):
            acc = ins[at][0].astype(F32)
            for i in range(1, parts):
                acc = acc + ins[at + i][0].astype(F32)
            at += parts
            out[:, c, :, h * width : (h + 1) * width] = acc


def local(cotangent, saved_gate_up, route_ids, route_weights, w_down):
    tokens, top = route_ids.shape
    width = cotangent.shape[1]
    units = saved_gate_up.shape[2] // 2
    nd, ne = lax.axis_size("dp"), lax.axis_size("expert")
    per, size = w_down.shape[0], w_down.shape[1]
    routes = tokens * top
    chunks = 2 if (size // 2) % ROWS == 0 else 1
    part = size // chunks
    bits = ne.bit_length() - 1
    groups = ne // 2
    held = groups * per
    p = lax.axis_index("dp").astype(jnp.int32)
    q = lax.axis_index("expert").astype(jnp.int32)
    pos = p.reshape(1)

    def owner_of(r):
        return ((q // 2) ^ r) * 2 + q % 2

    def swap(a, mask):
        return lax.ppermute(a, "expert", [(i, i ^ mask) for i in range(ne)])

    def shift(a, s):
        return lax.ppermute(a, "dp", [(i, (i + s) % nd) for i in range(nd)])

    eids = jnp.stack([owner_of(r) * per + e for r in range(groups) for e in range(per)]).astype(F32)

    gu = saved_gate_up.reshape(routes, 2 * units)
    wt = route_weights.T

    names = jnp.zeros((tokens, 128 * -(-tokens // 128)), BF16).at[:top, :tokens].set(route_ids.T.astype(BF16))
    sent = jnp.concatenate([cotangent, names], 1)

    def after(a, *done):
        return lax.optimization_barrier((a,) + done)[0]

    block = routes // 8
    shapes = []
    for s in range(nd):
        for c in range(chunks):
            shapes.append(jax.ShapeDtypeStruct((1, part, routes), BF16))
    whole = lambda shape: pl.BlockSpec(shape, lambda i: (0,) * len(shape))
    made = call(
        functools.partial(hidden_body, nd, top, chunks),
        0,
        6 * units * routes * 4,
        2 * (4 * block * units + 4 * units * routes),
        grid=(8,),
        in_specs=[SMEM, pl.BlockSpec((block, 2 * units), lambda i: (i, 0)), whole((top, tokens))],
        out_specs=[whole(o.shape) for o in shapes] + [whole((units, routes))],
        out_shape=shapes + [jax.ShapeDtypeStruct((units, routes), BF16)],
        scratch_shapes=[pltpu.VMEM((units // 128, routes, 128), F32), pltpu.VMEM((nd, size, routes), BF16)],
    )(pos, gu, wt)
    keep = made[-1]
    hs = [[made[s * chunks + c] for s in range(nd)] for c in range(chunks)]

    def back(weights, cots, ng, known, befores):
        nw, nc, count = len(weights), len(cots), sum(w.shape[0] for w in weights)
        n = sum(a.shape[0] for a in cots)
        blocks = n // tokens
        return call(
            functools.partial(back_body, nw, nc, ng, known, top),
            2 * count * size * width * n,
            2 * (count * size * width + n * width + n * top * size),
            2 * 2 * blocks * size * routes,
            in_specs=[SMEM] + [ANY] * (nw + nc + len(befores)),
            out_specs=[VMEM] * ng,
            out_shape=[jax.ShapeDtypeStruct((blocks // ng, size, routes), BF16)] * ng,
            scratch_shapes=[
                pltpu.VMEM((count, size, width), BF16),
                pltpu.VMEM((n, width), BF16),
                pltpu.VMEM((blocks, ROWS, tokens), BF16),
                pltpu.VMEM((blocks, top, ROWS, tokens), BF16),
                pltpu.VMEM((count, size, n), BF16),
                pltpu.VMEM((befores[0].shape[0] if befores else 1, size, routes), BF16),
                pltpu.SemaphoreType.DMA((nc + blocks + nw + 1,)),
            ],
        )(eids[:count], *weights, *cots, *befores)

    def pack(*lists):
        flat = [a for arrays in lists for a in arrays]
        shapes = [(sum(a.shape[0] for a in arrays),) + arrays[0].shape[1:] for arrays in lists]
        return call(
            functools.partial(pack_body, tuple(len(arrays) for arrays in lists)),
            0,
            4 * sum(a.size for a in flat),
            0,
            in_specs=[ANY] * len(flat),
            out_specs=[ANY] * len(lists),
            out_shape=[jax.ShapeDtypeStruct(shape, BF16) for shape in shapes],
            scratch_shapes=[pltpu.SemaphoreType.DMA((len(flat),))],
        )(*flat)

    far_step = nd // 2
    order = [0] + [s for s in range(1, nd) if s != far_step] + [far_step]
    first = after(w_down, sent)
    near = [swap(first, 2), swap(first, 4)] if bits == 3 else []
    far = {s: shift(sent, s) for s in range(1, nd) if s != far_step}
    moved = {far_step: shift(hs[0][far_step], far_step)}
    near, far, moved, hs, keep, sent = lax.optimization_barrier((near, far, moved, hs, keep, sent))

    if bits == 3:
        corner = [swap(near[0][: per // 2], 4), swap(near[1][per // 2 :], 2)]
        weights = [w_down] + near + corner
    else:
        weights = w_down
        for b in range(1, bits):
            weights = jnp.concatenate([weights, swap(weights, 1 << b)], 0)
        weights = [weights]
    far[far_step] = shift(far[far_step - 1], 1)
    for s in range(1, nd):
        if s != far_step:
            moved[s] = shift(hs[0][s], s)
    early = jnp.concatenate([sent] + [far[s] for s in order[1:-1]], 0)
    known = 3 if bits == 3 else 0
    begun = back(weights[:3], [early], 1, 0, []) if known else []
    weights, far, moved, hs, early, begun = lax.optimization_barrier((weights, far, moved, hs, early, begun))
    cots, packed = pack([early, far[far_step]], [hs[0][0]] + [moved[s] for s in order[1:]])
    mine = [packed]

    def send(c):
        return [hs[c][0]] + [shift(hs[c][s], s) for s in order[1:]]

    half = width // 2
    if bits == 3:
        plan = [((1, 3), 0, half), ((0, 2), 0, half), ((2, 3), half, width), ((0, 1), half, width)]
    else:
        plan = [(tuple(range(groups)), 0, width)]
    nb = 2 * nd
    columns = 512

    def down(eids, c):
        return call(
            functools.partial(down_body, top, plan, columns),
            2 * held * part * width * nb * tokens,
            2 * (held * part * width + nb * tokens * width + nb * routes * part),
            0,
            in_specs=[SMEM] + [ANY] * 4,
            out_specs=[ANY] * len(plan),
            out_shape=[jax.ShapeDtypeStruct((len(g), per, part, b - a), BF16) for g, a, b in plan],
            scratch_shapes=[
                pltpu.VMEM((nb * tokens, width), BF16),
                pltpu.VMEM((nb, part, routes), BF16),
                pltpu.VMEM((nb, ROWS, tokens), BF16),
                pltpu.VMEM((nb, top, step_of(part), tokens), BF16),
                pltpu.VMEM((held, part, nb * tokens), BF16),
                pltpu.VMEM((width // columns, held, part, columns), BF16),
                pltpu.SemaphoreType.DMA((4 + nb + width // columns * groups,)),
            ],
        )(eids, cots, cots_theirs, mine[c], theirs[c])

    cots_theirs = swap(cots, 1)
    theirs = [swap(mine[0], 1)]
    for c in range(1, chunks):
        mine.append(send(c))
    own, other = back(weights, [cots, cots_theirs], 2, known, begun)
    cots, cots_theirs, mine, theirs, own, other = lax.optimization_barrier(
        (cots, cots_theirs, mine, theirs, own, other)
    )

    other = swap(other, 1)
    for c in range(1, chunks):
        mine[c] = jnp.concatenate(mine[c], 0)
        theirs.append(swap(mine[c], 1))
    sums = [down(eids, 0)]
    cots, cots_theirs, mine, theirs, own, other, sums = lax.optimization_barrier(
        (cots, cots_theirs, mine, theirs, own, other, sums)
    )

    def middle(parts, got):
        return [(parts[i][1:].astype(F32) + a[1:2].astype(F32)).astype(BF16) for i, a in zip((1, 3), got)]

    plane = bits == 3
    got = [[swap(sums[0][0], 2), swap(sums[0][2], 4)]] if plane else []
    backs = [own[order.index(s)] + other[order.index(s)] for s in range(nd)]
    backs[1] = shift(backs[1], nd - 1)
    for c in range(1, chunks):
        sums.append(down(eids, c))
    sums, got, backs = lax.optimization_barrier((sums, got, backs))

    backs = [a if s < 2 else shift(a, nd - s) for s, a in enumerate(backs)]
    mids = []
    for c in range(1, chunks if plane else 1):
        mids = middle(sums[c - 1], got[c - 1])
        got.append(
            [
                swap(jnp.concatenate([sums[c][0], mids[1]], 0), 2),
                swap(jnp.concatenate([sums[c][2], mids[0]], 0), 4),
            ]
        )
        sums, got, backs = lax.optimization_barrier((sums, got, backs))

    terms = []
    if plane:
        mids = middle(sums[-1], got[-1])
        ends = [swap(mids[0], 4), swap(mids[1], 2)]
        for c in range(chunks):
            for i in range(2):
                end = (ends[i], 0) if c == chunks - 1 else (got[c + 1][1 - i], 2)
                terms += [(sums[c][2 * i + 1], 0), (got[c][i], 0), end]
    else:
        for parts in sums:
            acc = parts[0]
            for b in reversed(range(1, bits)):
                n = acc.shape[0] // 2
                acc = (acc[:n].astype(F32) + swap(acc[n:], 1 << b).astype(F32)).astype(BF16)
            terms.append((acc, 0))
    halves, parts = (2, 3) if bits == 3 else (1, 1)
    rows = part // 2 if part % (2 * ROWS) == 0 else part
    grad_down = call(
        functools.partial(total_body, chunks, halves, parts),
        0,
        2 * 5 * per * size * width,
        2 * per * rows * width * (2 * parts + 4) * chunks,
        grid=(part // rows,),
        in_specs=[
            pl.BlockSpec((1, per, rows, width // halves), lambda j, at=at: (at, 0, j, 0)) for _, at in terms
        ],
        out_specs=pl.BlockSpec((per, chunks, rows, width), lambda j: (0, 0, j, 0)),
        out_shape=jax.ShapeDtypeStruct((per, chunks, part, width), F32),
    )(*[a for a, _ in terms]).reshape(per, size, width)

    cols = units // 128
    out, route = call(
        functools.partial(final_body, nd, top),
        0,
        8 * units * routes * 4,
        2 * (2 * units * routes + 3 * 2 * 128 * routes),
        grid=(cols,),
        in_specs=[SMEM]
        + [whole((size, routes))] * nd
        + [
            pl.BlockSpec((routes, 128), lambda i: (0, i)),
            pl.BlockSpec((routes, 128), lambda i: (0, cols + i)),
            whole((top, tokens)),
            pl.BlockSpec((128, routes), lambda i: (i, 0)),
        ],
        out_specs=[ANY, whole((top, tokens))],
        out_shape=[
            jax.ShapeDtypeStruct((routes, 2 * units), BF16),
            jax.ShapeDtypeStruct((top, tokens), F32),
        ],
        scratch_shapes=[
            pltpu.VMEM((units, routes), BF16),
            pltpu.VMEM((routes, 128), F32),
            pltpu.VMEM((2, 2, routes, 128), BF16),
            pltpu.SemaphoreType.DMA((2, 2)),
        ],
    )(pos, *backs, gu, gu, wt, keep)
    return out.reshape(tokens, top, 2 * units), route.T, grad_down


def solution(mesh):
    return jax.shard_map(
        local,
        mesh=mesh,
        in_specs=(
            P(("dp", "expert"), None),
            P(("dp", "expert"), None, None),
            P(("dp", "expert"), None),
            P(("dp", "expert"), None),
            P("expert", "dp", None),
        ),
        out_specs=(
            P(("dp", "expert"), None, None),
            P(("dp", "expert"), None),
            P("expert", "dp", None),
        ),
        check_vma=False,
    )
```

```python
import functools
import math

import jax
import jax.numpy as jnp
from jax import lax
from jax.experimental import pallas as pl
from jax.experimental.pallas import tpu as pltpu
from jax.sharding import PartitionSpec as P

BF16 = jnp.bfloat16
F32 = jnp.float32
ANY = pl.BlockSpec(memory_space=pl.ANY)
VMEM = pl.BlockSpec(memory_space=pltpu.VMEM)
SMEM = pl.BlockSpec(memory_space=pltpu.SMEM)
MIB = 1024 * 1024
ROWS = 16


def call(kernel, flops, moved, windows, **kw):
    need = windows
    for buffer in kw.get("scratch_shapes", ()):
        if jnp.issubdtype(buffer.dtype, jnp.floating):
            need += math.prod(buffer.shape) * jnp.dtype(buffer.dtype).itemsize
    return pl.pallas_call(
        kernel,
        compiler_params=pltpu.CompilerParams(vmem_limit_bytes=(26 if need < 22 * MIB else 56) * MIB),
        cost_estimate=pl.CostEstimate(flops=int(flops), bytes_accessed=int(moved), transcendentals=0),
        **kw,
    )


def hidden_body(nd, top, chunks, pos, gu, wt, *rest):
    outs, keep, rows, packed = rest[: nd * chunks], rest[nd * chunks], rest[-2], rest[-1]
    step = pl.program_id(0)
    block, units = gu.shape[0], gu.shape[1] // 2
    g = gu[:, :units].astype(F32)
    u = gu[:, units:].astype(F32)
    h = g * jax.nn.sigmoid(g) * u
    for c in range(units // 128):
        rows[c, pl.ds(pl.multiple_of(step * block, block), block), :] = h[:, c * 128 : (c + 1) * 128]

    @pl.when(step == pl.num_programs(0) - 1)
    def _():
        tokens = wt.shape[1]
        slice_units = packed.shape[1]
        for k in range(top):
            for c in range(units // 128):
                part = rows[c, pl.ds(k, tokens, stride=top), :]
                part = part.T.astype(BF16)
                keep[c * 128 : (c + 1) * 128, k * tokens : (k + 1) * tokens] = part
        for z in range(nd):
            for k in range(top):
                w = wt[k : k + 1, :]
                part = keep[z * slice_units : (z + 1) * slice_units, k * tokens : (k + 1) * tokens]
                packed[z, :, k * tokens : (k + 1) * tokens] = (part.astype(F32) * w).astype(BF16)
        size = slice_units // chunks
        for s in range(nd):
            z = lax.rem(pos[0] + s, nd)
            for c in range(chunks):
                outs[s * chunks + c][0, :size, :] = packed[z, c * size : (c + 1) * size, :]


def spread(names, idv, top):
    for b in range(idv.shape[0]):
        rows = names[b].astype(F32)
        for k in range(top):
            idv[b, k] = jnp.broadcast_to(rows[k : k + 1, :], idv.shape[2:]).astype(BF16)


def step_of(units):
    return 2 * ROWS if units % (2 * ROWS) == 0 else ROWS


def tagged(eids, tokens, step=ROWS):
    return [jnp.full((step, tokens), eids[e], F32).astype(BF16) for e in range(eids.shape[0])]


def pack_body(counts, *refs):
    ins, outs, sem = refs[: sum(counts)], refs[sum(counts) : -1], refs[-1]
    copies = []
    for count, out in zip(counts, outs):
        at = 0
        for a in ins[len(copies) : len(copies) + count]:
            dst = out.at[pl.ds(at, a.shape[0])]
            copies.append(pltpu.make_async_copy(a, dst, sem.at[len(copies)]))
            at += a.shape[0]
    for c in copies:
        c.start()
    for c in copies:
        c.wait()


def back_body(nw, nc, ng, known, top, eids, *refs):
    ws, cots, refs = refs[:nw], refs[nw : nw + nc], refs[nw + nc :]
    befores, refs = refs[: known > 0], refs[known > 0 :]
    outs, (wv, cv, nv, idv, grads, pv, sem) = refs[:ng], refs[ng:]
    units, width = wv.shape[1:]
    blocks, tokens = idv.shape[0], idv.shape[3]
    per = blocks // ng
    done = befores[0].shape[0] if known else 0
    ready, copies, block = [], [], 0
    for i, cot in enumerate(cots):
        count = cot.shape[0] // tokens
        rows = pl.ds(block * tokens, count * tokens)
        ready.append(pltpu.make_async_copy(cot.at[:, pl.ds(0, width)], cv.at[rows, :], sem.at[i]))
        for b in range(count):
            src = cot.at[pl.ds(b * tokens, ROWS), pl.ds(width, tokens)]
            ready.append(pltpu.make_async_copy(src, nv.at[block + b], sem.at[nc + block + b]))
        block += count
    at, places = 0, []
    for i, w in enumerate(ws):
        places.append((at, w.shape[0]))
        copies.append(pltpu.make_async_copy(w, wv.at[pl.ds(at, w.shape[0])], sem.at[nc + blocks + i]))
        at += w.shape[0]
    for a in befores:
        copies.append(pltpu.make_async_copy(a, pv, sem.at[nc + blocks + nw]))
    for c in ready + copies:
        c.start()
    for c in ready:
        c.wait()
    spread(nv, idv, top)
    tags = tagged(eids, tokens)
    for i, (start, count) in enumerate(places):
        copies[i].wait()
        low = done * tokens if i < known else 0
        w = wv[start : start + count].reshape(count * units, width)
        got = lax.dot_general(w, cv[low:, :], (((1,), (1,)), ((), ())), preferred_element_type=F32)
        grads[start : start + count, :, low:] = got.astype(BF16).reshape(count, units, blocks * tokens - low)
    for c in copies[nw:]:
        c.wait()
    for block in range(blocks):
        cols = slice(block * tokens, (block + 1) * tokens)
        begun = block < done
        begin = places[known][0] if begun else 0

        def body(j, _, block=block, cols=cols, begun=begun, begin=begin):
            f = pl.multiple_of(j * ROWS, ROWS)
            held = {e: grads[e, pl.ds(f, ROWS), cols] for e in range(begin, at)}
            for k in range(top):
                span = slice(k * tokens, (k + 1) * tokens)
                row = idv[block, k]
                acc = pv[block, pl.ds(f, ROWS), span] if begun else jnp.zeros((ROWS, tokens), BF16)
                for e in held:
                    acc = jnp.where(row == tags[e], held[e], acc)
                outs[block // per][block % per, pl.ds(f, ROWS), span] = acc
            return 0

        lax.fori_loop(0, units // ROWS, body, 0)


def down_body(top, plan, columns, eids, *refs):
    cots, hs, outs = refs[:2], refs[2:4], refs[4 : 4 + len(plan)]
    cv, hv, nv, idv, dense, result, sem = refs[4 + len(plan) :]
    experts, units = dense.shape[:2]
    nb, tokens = idv.shape[0], idv.shape[3]
    half = nb // 2
    width = cv.shape[1]
    early, late = [], []
    for i in range(2):
        early.append(pltpu.make_async_copy(hs[i], hv.at[pl.ds(i * half, half)], sem.at[i]))
        for b in range(half):
            src = cots[i].at[pl.ds(b * tokens, ROWS), pl.ds(width, tokens)]
            early.append(pltpu.make_async_copy(src, nv.at[i * half + b], sem.at[4 + i * half + b]))
        src = cots[i].at[:, pl.ds(0, width)]
        late.append(pltpu.make_async_copy(src, cv.at[pl.ds(i * half * tokens, half * tokens), :], sem.at[2 + i]))
    for c in early:
        c.start()
    for c in early:
        c.wait()
    for c in late:
        c.start()
    spread(nv, idv, top)
    step = idv.shape[2]
    tags = tagged(eids, tokens, step)
    for b in range(nb):
        cols = slice(b * tokens, (b + 1) * tokens)

        def body(j, _, b=b, cols=cols):
            f = pl.multiple_of(j * step, ROWS)
            held = [hv[b, pl.ds(f, step), k * tokens : (k + 1) * tokens] for k in range(top)]
            rows = [idv[b, k] for k in range(top)]
            for e in range(experts):
                acc = jnp.zeros((step, tokens), BF16)
                for k in range(top):
                    acc = jnp.where(rows[k] == tags[e], held[k], acc)
                dense[e, pl.ds(f, step), cols] = acc
            return 0

        lax.fori_loop(0, units // step, body, 0)
    for c in late:
        c.wait()
    lhs = dense[...].reshape(experts * units, nb * tokens)
    copies = []
    for t, start in enumerate(range(0, width, columns)):
        got = jnp.dot(lhs, cv[:, start : start + columns], preferred_element_type=F32)
        result[t] = got.astype(BF16).reshape(experts, units, columns)
        for out, (groups, low, high) in zip(outs, plan):
            if low <= start < high:
                per = out.shape[1]
                for i, r in enumerate(groups):
                    dst = out.at[i, :, :, pl.ds(start - low, columns)]
                    src = result.at[t, pl.ds(r * per, per)]
                    copies.append(pltpu.make_async_copy(src, dst, sem.at[4 + nb + len(copies)]))
                    copies[-1].start()
    for c in copies:
        c.wait()


def final_body(nd, top, pos, *refs):
    backs, (g_ref, u_ref, wt, keep, out, route, turned, rows, held, sem) = refs[:nd], refs[nd:]
    step = pl.program_id(0)
    last = pl.num_programs(0) - 1
    tokens = wt.shape[1]
    units = turned.shape[0]

    @pl.when(step == 0)
    def _():
        size = backs[0].shape[0]
        for s in range(nd):
            at = pl.multiple_of(lax.rem(pos[0] + s, nd) * size, ROWS)
            turned[pl.ds(at, size), :] = backs[s][...]
        route[...] = jnp.zeros_like(route)

    f = pl.multiple_of(step * 128, 128)

    def copies(n):
        slot = lax.rem(n, 2)
        for i in range(2):
            col = pl.multiple_of(i * units + n * 128, 128)
            yield pltpu.make_async_copy(held.at[slot, i], out.at[:, pl.ds(col, 128)], sem.at[slot, i])

    for k in range(top):
        span = slice(k * tokens, (k + 1) * tokens)
        q = turned[pl.ds(f, 128), span].astype(F32)
        route[k : k + 1, :] += jnp.sum(q * keep[:, span].astype(F32), axis=0, keepdims=True)
        rows[pl.ds(k, tokens, stride=top), :] = (q * wt[k : k + 1, :]).T

    @pl.when(step >= 2)
    def _():
        for c in copies(step - 2):
            c.wait()

    slot = lax.rem(step, 2)
    g = g_ref[...].astype(F32)
    u = u_ref[...].astype(F32)
    d = rows[...]
    sig = jax.nn.sigmoid(g)
    held[slot, 0] = (d * u * sig * (1.0 + g * (1.0 - sig))).astype(BF16)
    held[slot, 1] = (d * (g * sig)).astype(BF16)
    for c in copies(step):
        c.start()

    @pl.when(step == last)
    def _():
        for n in (last - 1, last):
            for c in copies(n):
                c.wait()


def total_body(chunks, halves, parts, *refs):
    ins, out = refs[:-1], refs[-1]
    width = out.shape[3] // halves
    at = 0
    for c in range(chunks):
        for h in range(halves):
            acc = ins[at][0].astype(F32)
            for i in range(1, parts):
                acc = acc + ins[at + i][0].astype(F32)
            at += parts
            out[:, c, :, h * width : (h + 1) * width] = acc


def local(cotangent, saved_gate_up, route_ids, route_weights, w_down):
    tokens, top = route_ids.shape
    width = cotangent.shape[1]
    units = saved_gate_up.shape[2] // 2
    nd, ne = lax.axis_size("dp"), lax.axis_size("expert")
    per, size = w_down.shape[0], w_down.shape[1]
    routes = tokens * top
    chunks = 2 if (size // 2) % ROWS == 0 else 1
    part = size // chunks
    bits = ne.bit_length() - 1
    groups = ne // 2
    held = groups * per
    p = lax.axis_index("dp").astype(jnp.int32)
    q = lax.axis_index("expert").astype(jnp.int32)
    pos = p.reshape(1)

    def owner_of(r):
        return ((q // 2) ^ r) * 2 + q % 2

    def swap(a, mask):
        return lax.ppermute(a, "expert", [(i, i ^ mask) for i in range(ne)])

    def shift(a, s):
        return lax.ppermute(a, "dp", [(i, (i + s) % nd) for i in range(nd)])

    eids = jnp.stack([owner_of(r) * per + e for r in range(groups) for e in range(per)]).astype(F32)

    gu = saved_gate_up.reshape(routes, 2 * units)
    wt = route_weights.T

    names = jnp.zeros((tokens, 128 * -(-tokens // 128)), BF16).at[:top, :tokens].set(route_ids.T.astype(BF16))
    sent = jnp.concatenate([cotangent, names], 1)

    def after(a, *done):
        return lax.optimization_barrier((a,) + done)[0]

    block = routes // 8
    shapes = []
    for s in range(nd):
        for c in range(chunks):
            shapes.append(jax.ShapeDtypeStruct((1, part, routes), BF16))
    whole = lambda shape: pl.BlockSpec(shape, lambda i: (0,) * len(shape))
    made = call(
        functools.partial(hidden_body, nd, top, chunks),
        0,
        6 * units * routes * 4,
        2 * (4 * block * units + 4 * units * routes),
        grid=(8,),
        in_specs=[SMEM, pl.BlockSpec((block, 2 * units), lambda i: (i, 0)), whole((top, tokens))],
        out_specs=[whole(o.shape) for o in shapes] + [whole((units, routes))],
        out_shape=shapes + [jax.ShapeDtypeStruct((units, routes), BF16)],
        scratch_shapes=[pltpu.VMEM((units // 128, routes, 128), F32), pltpu.VMEM((nd, size, routes), BF16)],
    )(pos, gu, wt)
    keep = made[-1]
    hs = [[made[s * chunks + c] for s in range(nd)] for c in range(chunks)]

    def back(weights, cots, ng, known, befores):
        nw, nc, count = len(weights), len(cots), sum(w.shape[0] for w in weights)
        n = sum(a.shape[0] for a in cots)
        blocks = n // tokens
        return call(
            functools.partial(back_body, nw, nc, ng, known, top),
            2 * count * size * width * n,
            2 * (count * size * width + n * width + n * top * size),
            2 * 2 * blocks * size * routes,
            in_specs=[SMEM] + [ANY] * (nw + nc + len(befores)),
            out_specs=[VMEM] * ng,
            out_shape=[jax.ShapeDtypeStruct((blocks // ng, size, routes), BF16)] * ng,
            scratch_shapes=[
                pltpu.VMEM((count, size, width), BF16),
                pltpu.VMEM((n, width), BF16),
                pltpu.VMEM((blocks, ROWS, tokens), BF16),
                pltpu.VMEM((blocks, top, ROWS, tokens), BF16),
                pltpu.VMEM((count, size, n), BF16),
                pltpu.VMEM((befores[0].shape[0] if befores else 1, size, routes), BF16),
                pltpu.SemaphoreType.DMA((nc + blocks + nw + 1,)),
            ],
        )(eids[:count], *weights, *cots, *befores)

    def pack(*lists):
        flat = [a for arrays in lists for a in arrays]
        shapes = [(sum(a.shape[0] for a in arrays),) + arrays[0].shape[1:] for arrays in lists]
        return call(
            functools.partial(pack_body, tuple(len(arrays) for arrays in lists)),
            0,
            4 * sum(a.size for a in flat),
            0,
            in_specs=[ANY] * len(flat),
            out_specs=[ANY] * len(lists),
            out_shape=[jax.ShapeDtypeStruct(shape, BF16) for shape in shapes],
            scratch_shapes=[pltpu.SemaphoreType.DMA((len(flat),))],
        )(*flat)

    far_step = nd // 2
    order = [0] + [s for s in range(1, nd) if s != far_step] + [far_step]
    first = after(w_down, sent)
    near = [swap(first, 2), swap(first, 4)] if bits == 3 else []
    far = {s: shift(sent, s) for s in range(1, nd) if s != far_step}
    moved = {far_step: shift(hs[0][far_step], far_step)}
    near, far, moved, hs, keep, sent = lax.optimization_barrier((near, far, moved, hs, keep, sent))

    if bits == 3:
        corner = [swap(near[0][: per // 2], 4), swap(near[1][per // 2 :], 2)]
        weights = [w_down] + near + corner
    else:
        weights = w_down
        for b in range(1, bits):
            weights = jnp.concatenate([weights, swap(weights, 1 << b)], 0)
        weights = [weights]
    far[far_step] = shift(far[far_step - 1], 1)
    for s in range(1, nd):
        if s != far_step:
            moved[s] = shift(hs[0][s], s)
    early = jnp.concatenate([sent] + [far[s] for s in order[1:-1]], 0)
    known = 3 if bits == 3 else 0
    begun = back(weights[:3], [early], 1, 0, []) if known else []
    weights, far, moved, hs, early, begun = lax.optimization_barrier((weights, far, moved, hs, early, begun))
    cots, packed = pack([early, far[far_step]], [hs[0][0]] + [moved[s] for s in order[1:]])
    mine = [packed]

    def send(c):
        return [hs[c][0]] + [shift(hs[c][s], s) for s in order[1:]]

    half = width // 2
    if bits == 3:
        plan = [((1, 3), 0, half), ((0, 2), 0, half), ((2, 3), half, width), ((0, 1), half, width)]
    else:
        plan = [(tuple(range(groups)), 0, width)]
    nb = 2 * nd
    columns = 512

    def down(eids, c):
        return call(
            functools.partial(down_body, top, plan, columns),
            2 * held * part * width * nb * tokens,
            2 * (held * part * width + nb * tokens * width + nb * routes * part),
            0,
            in_specs=[SMEM] + [ANY] * 4,
            out_specs=[ANY] * len(plan),
            out_shape=[jax.ShapeDtypeStruct((len(g), per, part, b - a), BF16) for g, a, b in plan],
            scratch_shapes=[
                pltpu.VMEM((nb * tokens, width), BF16),
                pltpu.VMEM((nb, part, routes), BF16),
                pltpu.VMEM((nb, ROWS, tokens), BF16),
                pltpu.VMEM((nb, top, step_of(part), tokens), BF16),
                pltpu.VMEM((held, part, nb * tokens), BF16),
                pltpu.VMEM((width // columns, held, part, columns), BF16),
                pltpu.SemaphoreType.DMA((4 + nb + width // columns * groups,)),
            ],
        )(eids, cots, cots_theirs, mine[c], theirs[c])

    cots_theirs = swap(cots, 1)
    theirs = [swap(mine[0], 1)]
    for c in range(1, chunks):
        mine.append(send(c))
    own, other = back(weights, [cots, cots_theirs], 2, known, begun)
    cots, cots_theirs, mine, theirs, own, other = lax.optimization_barrier(
        (cots, cots_theirs, mine, theirs, own, other)
    )

    other = swap(other, 1)
    for c in range(1, chunks):
        mine[c] = jnp.concatenate(mine[c], 0)
        theirs.append(swap(mine[c], 1))
    sums = [down(eids, 0)]
    cots, cots_theirs, mine, theirs, own, other, sums = lax.optimization_barrier(
        (cots, cots_theirs, mine, theirs, own, other, sums)
    )

    def middle(parts, got):
        return [(parts[i][1:].astype(F32) + a[1:2].astype(F32)).astype(BF16) for i, a in zip((1, 3), got)]

    plane = bits == 3
    got = [[swap(sums[0][0], 2), swap(sums[0][2], 4)]] if plane else []
    backs = [own[order.index(s)] + other[order.index(s)] for s in range(nd)]
    backs = [a if s in (0, far_step) else shift(a, nd - s) for s, a in enumerate(backs)]
    for c in range(1, chunks):
        sums.append(down(eids, c))
    sums, got, backs = lax.optimization_barrier((sums, got, backs))

    backs[far_step] = shift(backs[far_step], nd - far_step)
    mids = []
    for c in range(1, chunks if plane else 1):
        mids = middle(sums[c - 1], got[c - 1])
        got.append(
            [
                swap(jnp.concatenate([sums[c][0], mids[1]], 0), 2),
                swap(jnp.concatenate([sums[c][2], mids[0]], 0), 4),
            ]
        )
        sums, got, backs = lax.optimization_barrier((sums, got, backs))

    terms = []
    if plane:
        mids = middle(sums[-1], got[-1])
        ends = [swap(mids[0], 4), swap(mids[1], 2)]
        for c in range(chunks):
            for i in range(2):
                end = (ends[i], 0) if c == chunks - 1 else (got[c + 1][1 - i], 2)
                terms += [(sums[c][2 * i + 1], 0), (got[c][i], 0), end]
    else:
        for parts in sums:
            acc = parts[0]
            for b in reversed(range(1, bits)):
                n = acc.shape[0] // 2
                acc = (acc[:n].astype(F32) + swap(acc[n:], 1 << b).astype(F32)).astype(BF16)
            terms.append((acc, 0))
    halves, parts = (2, 3) if bits == 3 else (1, 1)
    rows = part // 2 if part % (2 * ROWS) == 0 else part
    grad_down = call(
        functools.partial(total_body, chunks, halves, parts),
        0,
        2 * 5 * per * size * width,
        2 * per * rows * width * (2 * parts + 4) * chunks,
        grid=(part // rows,),
        in_specs=[
            pl.BlockSpec((1, per, rows, width // halves), lambda j, at=at: (at, 0, j, 0)) for _, at in terms
        ],
        out_specs=pl.BlockSpec((per, chunks, rows, width), lambda j: (0, 0, j, 0)),
        out_shape=jax.ShapeDtypeStruct((per, chunks, part, width), F32),
    )(*[a for a, _ in terms]).reshape(per, size, width)

    cols = units // 128
    out, route = call(
        functools.partial(final_body, nd, top),
        0,
        8 * units * routes * 4,
        2 * (2 * units * routes + 3 * 2 * 128 * routes),
        grid=(cols,),
        in_specs=[SMEM]
        + [whole((size, routes))] * nd
        + [
            pl.BlockSpec((routes, 128), lambda i: (0, i)),
            pl.BlockSpec((routes, 128), lambda i: (0, cols + i)),
            whole((top, tokens)),
            pl.BlockSpec((128, routes), lambda i: (i, 0)),
        ],
        out_specs=[ANY, whole((top, tokens))],
        out_shape=[
            jax.ShapeDtypeStruct((routes, 2 * units), BF16),
            jax.ShapeDtypeStruct((top, tokens), F32),
        ],
        scratch_shapes=[
            pltpu.VMEM((units, routes), BF16),
            pltpu.VMEM((routes, 128), F32),
            pltpu.VMEM((2, 2, routes, 128), BF16),
            pltpu.SemaphoreType.DMA((2, 2)),
        ],
    )(pos, *backs, gu, gu, wt, keep)
    return out.reshape(tokens, top, 2 * units), route.T, grad_down


def solution(mesh):
    return jax.shard_map(
        local,
        mesh=mesh,
        in_specs=(
            P(("dp", "expert"), None),
            P(("dp", "expert"), None, None),
            P(("dp", "expert"), None),
            P(("dp", "expert"), None),
            P("expert", "dp", None),
        ),
        out_specs=(
            P(("dp", "expert"), None, None),
            P(("dp", "expert"), None),
            P("expert", "dp", None),
        ),
        check_vma=False,
    )
```
